768 devices in a mesh: gx: 12 (over z), gy: 4 (over x), gz: 16 (over y, core).
Axes of the slice: x: 4, y: 8, z: 12, core: 2. Of those that a mesh axis runs over, the one named last changes fastest.
Arguments:
- markers: float32 [4, 96, 256, 2048], P(None, 'gx', 'gy', 'gz'), may hold values from 0 to 1
- velocity: float32 [96, 256, 2048], P('gx', 'gy', 'gz'), may hold values from -0.45 to 0.45
- patch_boxes: int32 [4, 49152], P(None, ('gx', 'gy', 'gz')), may hold values from 0 to 96, as said below
- send_pick: int32 [12, 4, 16, 64, 2], P('gx', 'gy', 'gz'), may hold values from 0 to 63
- recv_pick: int32 [12, 4, 16, 64, 2], P('gx', 'gy', 'gz'), may hold values from 0 to 63
- pair_count: int32 [12, 4, 16, 64], P('gx', 'gy', 'gz'), may hold values from 0 to 2, as said below
Outputs:
- advected: float32 [4, 96, 256, 2048], P(None, 'gx', 'gy', 'gz')
- bubble_force: float32 [49152, 4096], P(('gx', 'gy', 'gz'))
The draws below stay inside these ranges and needn't reach their ends.
Inputs may be any that keep to these rules, and one draw needn't show every extreme that they name: `patch_boxes`: patch boxes lie inside their owner's block: first cells along x, y, z run to at most 4, 32, 96; the marker function is below 4. `pair_count`: A device's count to itself is 0; in every slab the first device has 2 pairs to every other peer.
All inputs are finite; a program needn't handle non-finite values.
Results may differ from the reference program's by a relative error of at most 0.005.
Values may be sent and summed in bfloat16 or wider, within the bound.
A program may use at most 32 MiB of HBM per device.

```python
import jax
import jax.numpy as jnp
from jax import lax

CX = 8
CY = 64
CZ = 128
B_DEV = 64
MARK = 4
BAND = 4
PATCH = 32
SLOT = 2
FLAT = 4096
PEERS = 64
NX = 96
NY = 256
NZ = 2048
BUBBLES = 49152
N_GX = 12
N_GY = 4
N_GZ = 16


def draw_patch_boxes(key, part):
    key = jax.random.fold_in(key, 11)
    keys = jax.random.split(key, 4)
    color = jax.random.randint(keys[0], (BUBBLES,), 0, MARK)
    start_x = jax.random.randint(keys[1], (BUBBLES,), 0, CX - BAND + 1)
    start_y = jax.random.randint(keys[2], (BUBBLES,), 0, CY - PATCH + 1)
    start_z = jax.random.randint(keys[3], (BUBBLES,), 0, CZ - PATCH + 1)
    leading = jnp.arange(BUBBLES) % B_DEV == 0
    start_z = jnp.where(leading, CZ - PATCH, start_z)
    return jnp.stack([color, start_x, start_y, start_z]).astype(jnp.int32)


def draw_pair_count(key, part):
    key = jax.random.fold_in(key, 23)
    keys = jax.random.split(key, 2)
    base = jax.random.randint(keys[0], (N_GX, N_GY, N_GZ, PEERS), 0, SLOT + 1)
    heavy = jax.random.randint(keys[1], (N_GX, N_GY, N_GZ, 1), 0, 4) == 0
    sender = jnp.arange(N_GY)[:, None] * N_GZ + jnp.arange(N_GZ)[None, :]
    heavy = heavy | (sender == 0)[None, :, :, None]
    counts = jnp.where(heavy, SLOT, base)
    itself = sender[None, :, :, None] == jnp.arange(PEERS)[None, None, None, :]
    return jnp.where(itself, 0, counts).astype(jnp.int32)


def set_ends(entries, own_key, smallest, largest):
    spot = [jax.random.randint(jax.random.fold_in(own_key, axis), (), 0, length) for axis, length in enumerate(entries.shape)]
    widest = entries.shape.index(max(entries.shape))
    beside = spot[:widest] + [(spot[widest] + 1) % entries.shape[widest]] + spot[widest + 1:]
    return entries.at[tuple(spot)].set(smallest).at[tuple(beside)].set(largest)


def steps_of(key, extent, pieces, least, high):
    factor_of = 1.0
    for axis_at, shards_of in pieces:
        steps = jax.random.uniform(jax.random.fold_in(jax.random.fold_in(key, 6), axis_at), (shards_of,), jnp.float32, least / len(pieces), high / len(pieces))
        factor_of = factor_of * jnp.repeat(jnp.exp(steps), extent[axis_at] // shards_of).reshape((-1,) + (1,) * (len(extent) - 1 - axis_at))
    return factor_of


def setup_inputs(seed: int = 0) -> dict:
    arg_keys = jax.random.split(jax.random.key(seed), 7)
    return {
        "markers": jnp.clip(1.0 * jax.random.uniform(arg_keys[0], (MARK, NX, NY, NZ), jnp.float32) ** steps_of(arg_keys[0], (MARK, NX, NY, NZ), ((1, 12), (2, 4), (3, 16)), -0.2, 0.2), 0.0, 1.0),
        "velocity": jnp.clip(jax.random.uniform(arg_keys[1], (NX, NY, NZ), jnp.float32, -0.45, 0.45) * steps_of(arg_keys[1], (NX, NY, NZ), ((0, 12), (1, 4), (2, 16)), -0.4, 0.0), -0.45, 0.45),
        "patch_boxes": draw_patch_boxes(jax.random.fold_in(arg_keys[6], 71), 0),
        "send_pick": set_ends(jax.random.randint(arg_keys[3], (N_GX, N_GY, N_GZ, PEERS, SLOT), 0, B_DEV), jax.random.fold_in(arg_keys[3], 1), 0, B_DEV - 1).astype(jnp.int32),
        "recv_pick": set_ends(jax.random.randint(arg_keys[4], (N_GX, N_GY, N_GZ, PEERS, SLOT), 0, B_DEV), jax.random.fold_in(arg_keys[4], 1), 0, B_DEV - 1).astype(jnp.int32),
        "pair_count": draw_pair_count(jax.random.fold_in(arg_keys[6], 71), 0),
    }


def advect_channel(channel, face):
    shifted = jnp.pad(channel, ((1, 1), (0, 0), (0, 0)))
    flux = face * jnp.where(face > 0, shifted[:-1], shifted[1:])
    return channel - (flux[1:] - flux[:-1]) + channel * (face[1:] - face[:-1])


def reference(markers, velocity, patch_boxes, send_pick, recv_pick, pair_count):
    padded_velocity = jnp.pad(velocity, ((1, 1), (0, 0), (0, 0)))
    face = 0.5 * (padded_velocity[:-1] + padded_velocity[1:])
    advected = lax.map(lambda channel: advect_channel(channel, face), markers)

    def slab_force(slab):
        first = slab * PEERS * B_DEV
        boxes = lax.dynamic_slice_in_dim(patch_boxes, first, PEERS * B_DEV, 1)
        owner = jnp.arange(PEERS * B_DEV, dtype=jnp.int32) // B_DEV
        anchor_x = boxes[1] + slab * CX
        anchor_y = boxes[2] + (owner // N_GZ) * CY
        anchor_z = boxes[3] + (owner % N_GZ) * CZ

        def one_patch(color, start_x, start_y, start_z):
            piece = lax.dynamic_slice(markers, (color, start_x, start_y, start_z), (1, BAND, PATCH, PATCH))
            return piece.reshape(FLAT).astype(jnp.bfloat16)

        patches = jax.vmap(one_patch)(boxes[0], anchor_x, anchor_y, anchor_z)
        picks_far = lax.dynamic_index_in_dim(send_pick, slab, 0, False).reshape(PEERS, PEERS, SLOT)
        picks_near = lax.dynamic_index_in_dim(recv_pick, slab, 0, False).reshape(PEERS, PEERS, SLOT)
        counts = lax.dynamic_index_in_dim(pair_count, slab, 0, False).reshape(PEERS, PEERS)
        source = jnp.arange(PEERS, dtype=jnp.int32)
        far_index = (source[:, None, None] * B_DEV + picks_far).reshape(-1)
        near_index = (source[None, :, None] * B_DEV + jnp.transpose(picks_near, (1, 0, 2))).reshape(-1)
        used = (jnp.arange(SLOT, dtype=jnp.int32)[None, None, :] < counts[:, :, None]).reshape(-1, 1)
        far = jnp.where(used, patches[far_index], jnp.zeros((1, FLAT), jnp.bfloat16))
        near = patches[near_index]
        near_wide = near.astype(jnp.float32)
        far_wide = far.astype(jnp.float32)
        film = 0.8 * near_wide * far_wide
        near_force = (film * (1.0 - near_wide)).astype(jnp.bfloat16)
        far_force = (film * (1.0 - far_wide)).astype(jnp.bfloat16)
        total = jax.ops.segment_sum(near_force.astype(jnp.float32), near_index, PEERS * B_DEV)
        total = total + jax.ops.segment_sum(far_force.astype(jnp.float32), far_index, PEERS * B_DEV)
        return total

    forces = lax.map(slab_force, jnp.arange(N_GX, dtype=jnp.int32))
    return advected, forces.reshape(BUBBLES, FLAT)
```

```python
import jax
import jax.numpy as jnp
from jax import lax
from jax.experimental import pallas as pl
from jax.experimental.pallas import tpu as pltpu
from jax.sharding import PartitionSpec as P

MESH = pl.DeviceIdType.MESH
BAND = 4
PATCH = 32
BUB = 64
NY = 8
NX = 4
NZ = 12
CHIPS = NX * NY
LANES = 128
UNUSED = 512.0
F32 = jnp.float32
BF16 = jnp.bfloat16


def cut_kernel(boxes, rows, out, tmp):
    lane = lax.broadcasted_iota(jnp.int32, (8, LANES), 1) // PATCH

    def one(b, _):
        base = (boxes[0, b] * 8 + boxes[1, b]) * 64 + boxes[2, b]
        z0 = boxes[3, b]
        for dx in range(BAND):
            cells = jnp.zeros((8, LANES), F32)
            for j in range(4):
                piece = rows[pl.ds(base + dx * 64 + j, 8, stride=4), :]
                piece = pltpu.roll(piece, lax.rem(PATCH * j - z0 + LANES, LANES), 1)
                cells = jnp.where(lane == j, piece, cells)
            tmp[pl.ds(pl.multiple_of(b * CHIPS + dx * 8, 8), 8), :] = cells
        return 0

    lax.fori_loop(0, BUB, one, 0)

    def put(s, _):
        out[s] = tmp[pl.ds(s, BUB, stride=CHIPS), :].astype(BF16)
        return 0

    lax.fori_loop(0, CHIPS, put, 0)


def cut(boxes, markers):
    return pl.pallas_call(
        cut_kernel,
        out_shape=jax.ShapeDtypeStruct((CHIPS, BUB, LANES), BF16),
        in_specs=[
            pl.BlockSpec(memory_space=pltpu.SMEM),
            pl.BlockSpec(memory_space=pltpu.VMEM),
        ],
        out_specs=pl.BlockSpec(memory_space=pltpu.VMEM),
        scratch_shapes=[pltpu.VMEM((BUB * CHIPS, LANES), F32)],
    )(boxes, markers.reshape(-1, LANES))


def step_of(j):
    k = j // 4
    m = 4 - (k + 1) // 2
    dy = lax.rem(m + (1 - lax.rem(k, 2)) * (8 - 2 * m), NY)
    dx = lax.rem(lax.rem(j, 4) + 1, NX)
    return dx, dy


def exchange_kernel(
    x_ref,
    p_ref,
    markers,
    velocity,
    adv,
    force,
    x_all,
    pall,
    fbuf,
    nbuf,
    g,
    ssend,
    srecv,
    mhalo,
    vhalo,
    x_send,
    x_recv,
    xs_sem,
    p_send,
    p_recv,
    ps_send,
    ps_recv,
    s_send,
    s_recv,
    h_send,
    h_recv,
):
    gx = lax.axis_index("gx")
    gy = lax.axis_index("gy")
    gz = lax.axis_index("gz")
    y = gz // 2
    c = lax.rem(gz, 2)
    h = y * NX + gy
    other = 1 - c
    sibling = (gx, gy, y * 2 + other)
    up = (lax.rem(gx + 1, NZ), gy, gz)
    down = (lax.rem(gx + NZ - 1, NZ), gy, gz)

    def target(j):
        dx, dy = step_of(j)
        ty, tx = lax.rem(y + dy, NY), lax.rem(gy + dx, NX)
        return ty * NX + tx, (gx, tx, ty * 2 + c)

    def source(j):
        dx, dy = step_of(j)
        ty, tx = lax.rem(y + NY - dy, NY), lax.rem(gy + NX - dx, NX)
        return ty * NX + tx

    barrier = pltpu.get_barrier_semaphore()

    def greet(j, _):
        pl.semaphore_signal(barrier, inc=1, device_id=target(j)[1], device_id_type=MESH)
        return 0

    lax.fori_loop(0, CHIPS - 1, greet, 0)
    for device in (sibling, up, down):
        pl.semaphore_signal(barrier, inc=1, device_id=device, device_id_type=MESH)
    pl.semaphore_wait(barrier, CHIPS - 1 + 3)

    def x_copy(to, device):
        return pltpu.make_async_remote_copy(
            src_ref=x_ref,
            dst_ref=x_all.at[c * CHIPS + h],
            send_sem=x_send.at[to],
            recv_sem=x_recv.at[h],
            device_id=device,
            device_id_type=MESH,
        )

    def p_copy(to, device):
        return pltpu.make_async_remote_copy(
            src_ref=p_ref.at[to],
            dst_ref=pall.at[c * CHIPS + h],
            send_sem=p_send.at[to],
            recv_sem=p_recv.at[h],
            device_id=device,
            device_id_type=MESH,
        )

    def s_copy(to, device):
        return pltpu.make_async_remote_copy(
            src_ref=ssend.at[to],
            dst_ref=srecv.at[h],
            send_sem=s_send.at[to],
            recv_sem=s_recv.at[h],
            device_id=device,
            device_id_type=MESH,
        )

    def x_landed(frm):
        return pltpu.make_async_remote_copy(
            src_ref=x_ref,
            dst_ref=x_all.at[c * CHIPS + frm],
            send_sem=x_send.at[frm],
            recv_sem=x_recv.at[frm],
            device_id=sibling,
            device_id_type=MESH,
        )

    def p_landed(frm):
        return pltpu.make_async_remote_copy(
            src_ref=p_ref.at[frm],
            dst_ref=pall.at[c * CHIPS + frm],
            send_sem=p_send.at[frm],
            recv_sem=p_recv.at[frm],
            device_id=sibling,
            device_id_type=MESH,
        )

    def s_landed(frm):
        return pltpu.make_async_remote_copy(
            src_ref=ssend.at[frm],
            dst_ref=srecv.at[frm],
            send_sem=s_send.at[frm],
            recv_sem=s_recv.at[frm],
            device_id=sibling,
            device_id_type=MESH,
        )

    halos = []
    for way, device, plane in ((0, up, 7), (1, down, 0)):
        halos.append(
            pltpu.make_async_remote_copy(
                src_ref=markers.at[:, plane],
                dst_ref=mhalo.at[way],
                send_sem=h_send.at[2 * way],
                recv_sem=h_recv.at[2 * way],
                device_id=device,
                device_id_type=MESH,
            )
        )
        halos.append(
            pltpu.make_async_remote_copy(
                src_ref=velocity.at[plane],
                dst_ref=vhalo.at[way],
                send_sem=h_send.at[2 * way + 1],
                recv_sem=h_recv.at[2 * way + 1],
                device_id=device,
                device_id_type=MESH,
            )
        )

    def send_x(j, _):
        x_copy(*target(j)).start()
        return 0

    def send_p(j, _):
        p_copy(*target(j)).start()
        return 0

    lax.fori_loop(0, CHIPS - 1, send_x, 0)
    lax.fori_loop(0, CHIPS - 1, send_p, 0)
    for copy in halos:
        copy.start()
    x_all[c * CHIPS + h] = x_ref[...]
    pall[c * CHIPS + h] = p_ref[h]

    def wait_x(j, _):
        x_landed(source(j)).wait_recv()
        return 0

    lax.fori_loop(0, CHIPS - 1, wait_x, 0)
    x_share = pltpu.make_async_remote_copy(
        src_ref=x_all.at[pl.ds(c * CHIPS, CHIPS)],
        dst_ref=x_all.at[pl.ds(c * CHIPS, CHIPS)],
        send_sem=xs_sem.at[0],
        recv_sem=xs_sem.at[1],
        device_id=sibling,
        device_id_type=MESH,
    )
    x_share.start()

    for copy in halos:
        copy.wait()
    low = jnp.where(gx == 0, 0.0, 1.0).astype(F32)
    high = jnp.where(gx == NZ - 1, 0.0, 1.0).astype(F32)

    def advect(t, _):
        rows = pl.ds(pl.multiple_of(t * 8, 8), 8)
        vel = [vhalo[0, rows, :] * low] + [velocity[i, rows, :] for i in range(8)]
        vel = vel + [vhalo[1, rows, :] * high]
        face = [0.5 * (vel[i] + vel[i + 1]) for i in range(9)]
        for m in range(4):
            mark = [mhalo[0, m, rows, :] * low] + [markers[m, i, rows, :] for i in range(8)]
            mark = mark + [mhalo[1, m, rows, :] * high]
            flux = [face[i] * jnp.where(face[i] > 0, mark[i], mark[i + 1]) for i in range(9)]
            for i in range(8):
                here = mark[i + 1]
                adv[m, i, rows, :] = (
                    here - (flux[i + 1] - flux[i]) + here * (face[i + 1] - face[i])
                )
        return 0

    lax.fori_loop(0, 8, advect, 0)

    x_share.wait()

    picks = jnp.where(c == 0, x_all[:, 0, :], x_all[:, 1, :]).astype(BF16)
    row = lax.broadcasted_iota(jnp.int32, (512, LANES), 0)
    lane = lax.broadcasted_iota(jnp.int32, (512, LANES), 1)
    spread = (row // 16 == lane // 4) & (lax.rem(row, 4) == lax.rem(lane, 4))
    wide = lax.dot_general(
        spread.astype(F32).astype(BF16),
        picks,
        (((1,), (1,)), ((), ())),
        preferred_element_type=F32,
    )
    row = lax.broadcasted_iota(jnp.int32, (512, 2 * CHIPS), 0)
    lane = lax.broadcasted_iota(jnp.int32, (512, 2 * CHIPS), 1)
    place = lane - lax.rem(row // 4, 4)
    ones = jnp.ones((2 * CHIPS, 4 * BUB), BF16)
    row = lax.broadcasted_iota(jnp.int32, (512, 4 * BUB), 0)
    lane = lax.broadcasted_iota(jnp.int32, (512, 4 * BUB), 1)
    wanted = (lane - BUB * lax.rem(row // 4, 4)).astype(F32)

    def gather_matrix(k, _):
        mine = jnp.where(place == 4 * k, wide, 0.0).astype(BF16)
        index = jnp.dot(mine, ones, preferred_element_type=F32)
        fbuf[k] = jnp.where(index == wanted, 1.0, 0.0).astype(BF16)
        return 0

    lax.fori_loop(0, 2 * NY, gather_matrix, 0)

    bubble = lax.broadcasted_iota(jnp.int32, (BUB, LANES), 0).astype(F32)
    first = lax.rem(lax.broadcasted_iota(jnp.int32, (1, LANES), 1), 4) < 2

    def sum_matrix(q, _):
        for core in range(2):
            index = x_all[c * CHIPS + q, pl.ds(core, 1), :]
            index = jnp.where(first, pltpu.roll(index, LANES - 2, 1), pltpu.roll(index, 2, 1))
            nbuf[q, :, core * LANES : (core + 1) * LANES] = jnp.where(
                bubble == index, 1.0, 0.0
            ).astype(BF16)
        return 0

    lax.fori_loop(0, CHIPS, sum_matrix, 0)

    def gather(block):
        patches = pall[pl.ds(block * 4, 4)].reshape(4 * BUB, LANES)
        partner = jnp.dot(fbuf[block], patches, preferred_element_type=F32)
        g[:, pl.ds(pl.multiple_of(block * 16, 16), 16), :] = partner.reshape(
            CHIPS, 16, LANES
        ).astype(BF16)

    def share(core, line):
        chips = pl.ds(core * CHIPS + line * 4, 4)
        return pltpu.make_async_remote_copy(
            src_ref=pall.at[chips],
            dst_ref=pall.at[chips],
            send_sem=ps_send.at[line],
            recv_sem=ps_recv.at[line],
            device_id=sibling,
            device_id_type=MESH,
        )

    def line_of(k):
        return source(4 * k) // NX

    def own_line(k, _):
        line = line_of(k)

        def wait_p(j, _):
            p_landed(source(j)).wait_recv()
            return 0

        lax.fori_loop(4 * k, lax.min(4 * k + 4, CHIPS - 1), wait_p, 0)
        share(c, line).start()
        gather(c * NY + line)
        return 0

    lax.fori_loop(0, NY, own_line, 0)

    def other_line(k, _):
        line = line_of(k)
        share(other, line).wait_recv()
        gather(other * NY + line)
        return 0

    lax.fori_loop(0, NY, other_line, 0)

    def sums(q):
        return jnp.dot(nbuf[q], g[q], preferred_element_type=F32).astype(BF16)

    def send_s(j, _):
        to, device = target(j)
        ssend[to] = sums(to)
        s_copy(to, device).start()
        return 0

    lax.fori_loop(0, CHIPS - 1, send_s, 0)
    srecv[h] = sums(h)

    def finish(at):
        patch = p_ref[at].astype(F32)
        lanes = pl.ds(pl.multiple_of(at * LANES, LANES), LANES)
        force[:, lanes] = 0.8 * patch * (1.0 - patch) * srecv[at].astype(F32)

    finish(h)

    def wait_s(j, _):
        frm = source(j)
        s_landed(frm).wait_recv()
        finish(frm)
        return 0

    lax.fori_loop(0, CHIPS - 1, wait_s, 0)

    def wait_sent(j, _):
        to, device = target(j)
        x_copy(to, device).wait_send()
        p_copy(to, device).wait_send()
        s_copy(to, device).wait_send()
        return 0

    lax.fori_loop(0, CHIPS - 1, wait_sent, 0)

    def wait_shared(line, _):
        share(c, line).wait_send()
        return 0

    lax.fori_loop(0, NY, wait_shared, 0)


def exchange(x, patches, markers, velocity):
    vmem = pl.BlockSpec(memory_space=pltpu.VMEM)
    dma = pltpu.SemaphoreType.DMA
    return pl.pallas_call(
        exchange_kernel,
        out_shape=(
            jax.ShapeDtypeStruct(markers.shape, F32),
            jax.ShapeDtypeStruct((BUB, CHIPS * LANES), F32),
        ),
        in_specs=[vmem] * 4,
        out_specs=[vmem] * 2,
        scratch_shapes=[
            pltpu.VMEM((2 * CHIPS, 2, LANES), F32),
            pltpu.VMEM((2 * CHIPS, BUB, LANES), BF16),
            pltpu.VMEM((2 * NY, 512, 4 * BUB), BF16),
            pltpu.VMEM((CHIPS, BUB, 2 * LANES), BF16),
            pltpu.VMEM((CHIPS, 4 * BUB, LANES), BF16),
            pltpu.VMEM((CHIPS, BUB, LANES), BF16),
            pltpu.VMEM((CHIPS, BUB, LANES), BF16),
            pltpu.VMEM((2, 4, 64, LANES), F32),
            pltpu.VMEM((2, 64, LANES), F32),
            dma((CHIPS,)),
            dma((CHIPS,)),
            dma((2,)),
            dma((CHIPS,)),
            dma((CHIPS,)),
            dma((NY,)),
            dma((NY,)),
            dma((CHIPS,)),
            dma((CHIPS,)),
            dma((4,)),
            dma((4,)),
        ],
        compiler_params=pltpu.CompilerParams(
            collective_id=0, has_side_effects=True, vmem_limit_bytes=40 * 1024 * 1024
        ),
    )(x, patches, markers, velocity)


def on_device(markers, velocity, patch_boxes, send_pick, recv_pick, pair_count):
    slots = send_pick.shape[-1]
    used = jnp.arange(slots, dtype=jnp.int32) < pair_count[..., None]
    sent = jnp.where(used, send_pick.astype(F32), UNUSED)
    x = jnp.concatenate([sent, recv_pick.astype(F32)], axis=-1)
    x = x.reshape(NX, NY, 2, 2 * slots).transpose(2, 1, 0, 3).reshape(2, LANES)
    patches = cut(patch_boxes, markers)
    return exchange(x, patches, markers, velocity)


def solution(mesh):
    placed = (
        P(None, "gx", "gy", "gz"),
        P("gx", "gy", "gz"),
        P(None, ("gx", "gy", "gz")),
        P("gx", "gy", "gz", None, None),
        P("gx", "gy", "gz", None, None),
        P("gx", "gy", "gz", None),
    )
    return jax.shard_map(
        on_device,
        mesh=mesh,
        in_specs=placed,
        out_specs=(P(None, "gx", "gy", "gz"), P(("gx", "gy", "gz"), None)),
        check_vma=False,
    )
```

```python
import jax
import jax.numpy as jnp
from jax import lax
from jax.experimental import pallas as pl
from jax.experimental.pallas import tpu as pltpu
from jax.sharding import PartitionSpec as P

MESH = pl.DeviceIdType.MESH
PATCH = 32
BUB = 64
NY = 8
NX = 4
NZ = 12
CHIPS = NX * NY
HALF = CHIPS // 2
PAIRS = CHIPS
LANES = 128
UNUSED = 512.0
F32 = jnp.float32
BF16 = jnp.bfloat16


def iota(shape, dim):
    return lax.broadcasted_iota(jnp.int32, shape, dim)


def chip_at(h):
    y = lax.rem(h, HALF) // 2
    return 2 * lax.rem(h, 2) + lax.rem(h // HALF + y, 2), y


def peer_at(h, core):
    gy, y = chip_at(h)
    return gy * 16 + y * 2 + core


def exchange_kernel(
    boxes_hbm,
    send_hbm,
    recv_hbm,
    count_hbm,
    markers_hbm,
    velocity_hbm,
    adv,
    force,
    boxes,
    send_pick,
    recv_pick,
    count,
    markers,
    velocity,
    tmp,
    ploc,
    x_msg,
    x_all,
    pall,
    fbuf,
    nidx,
    nbuf,
    g,
    ssend,
    srecv,
    mhalo,
    vhalo,
    in_sem,
    x_send,
    x_recv,
    xs_sem,
    p_send,
    p_recv,
    ps_send,
    ps_recv,
    s_send,
    s_recv,
    h_send,
    h_recv,
):
    gx = lax.axis_index("gx")
    gy = lax.axis_index("gy")
    gz = lax.axis_index("gz")
    y = gz // 2
    c = lax.rem(gz, 2)
    parity = lax.rem(gy + y, 2)
    h = parity * HALF + y * 2 + gy // 2
    other = 1 - c
    sibling = (gx, gy, y * 2 + other)
    up = (lax.rem(gx + 1, NZ), gy, gz)
    down = (lax.rem(gx + NZ - 1, NZ), gy, gz)

    loads = []
    for src, dst in (
        (boxes_hbm, boxes),
        (send_hbm, send_pick),
        (recv_hbm, recv_pick),
        (count_hbm, count),
        *((markers_hbm.at[m], markers.at[m]) for m in range(4)),
        (velocity_hbm, velocity),
    ):
        loads.append(pltpu.make_async_copy(src, dst, in_sem.at[len(loads)]))
        loads[-1].start()

    def row_step(k):
        m = 4 - (k + 1) // 2
        return lax.rem(m + (1 - lax.rem(k, 2)) * (8 - 2 * m), NY)

    def place(dx, dy):
        ty, tx = lax.rem(y + dy, NY), lax.rem(gy + dx, NX)
        number = lax.rem(tx + ty, 2) * HALF + ty * 2 + tx // 2
        return number, (gx, tx, ty * 2 + c)

    def target(j):
        return place(lax.rem(lax.rem(j, 4) + 1, NX), row_step(j // 4))

    def target_in(half, i):
        dy = row_step(i // 2)
        turn = lax.rem(half + parity + dy, 2)
        dx = turn + 2 * (1 - lax.rem(i, 2))
        return place(lax.rem(dx, NX), dy)

    barrier = pltpu.get_barrier_semaphore()

    def greet(j, _):
        pl.semaphore_signal(barrier, inc=1, device_id=target(j)[1], device_id_type=MESH)
        return 0

    lax.fori_loop(0, CHIPS - 1, greet, 0)
    for device in (sibling, up, down):
        pl.semaphore_signal(barrier, inc=1, device_id=device, device_id_type=MESH)

    for copy in loads:
        copy.wait()

    for s in range(2):
        far = jnp.where(count[...] > s, send_pick[s : s + 1, :].astype(F32), UNUSED)
        x_msg[s : s + 1, 0:BUB] = far
        x_msg[s : s + 1, BUB:LANES] = recv_pick[s : s + 1, :].astype(F32)

    group = iota((8, LANES), 1) // PATCH
    rows = markers.reshape(4 * 8 * 64, LANES)

    def cut(half):
        def one(b, _):
            base = (boxes[0, b] * 8 + boxes[1, b]) * 64 + boxes[2, b]
            z0 = boxes[3, b]
            for dx in range(2):
                cells = None
                for j in range(4):
                    piece = rows[pl.ds(base + (2 * half + dx) * 64 + j, 8, stride=4), :]
                    piece = pltpu.roll(piece, lax.rem(PATCH * j - z0 + LANES, LANES), 1)
                    cells = piece if j == 0 else jnp.where(group == j, piece, cells)
                tmp[pl.ds(pl.multiple_of(b * HALF + dx * 8, 8), 8), :] = cells
            return 0

        lax.fori_loop(0, BUB, one, 0, unroll=8)

        def put(s, _):
            ploc[half * HALF + s] = tmp[pl.ds(s, BUB, stride=HALF), :].astype(BF16)
            return 0

        lax.fori_loop(0, HALF, put, 0, unroll=4)

    cut(0)

    pl.semaphore_wait(barrier, CHIPS - 1 + 3)

    def x_copy(to, device):
        return pltpu.make_async_remote_copy(
            src_ref=x_msg,
            dst_ref=x_all.at[c * CHIPS + h],
            send_sem=x_send.at[to],
            recv_sem=x_recv.at[h],
            device_id=device,
            device_id_type=MESH,
        )

    def p_copy(to, device):
        return pltpu.make_async_remote_copy(
            src_ref=ploc.at[to],
            dst_ref=pall.at[c * CHIPS + h],
            send_sem=p_send.at[to],
            recv_sem=p_recv.at[h],
            device_id=device,
            device_id_type=MESH,
        )

    def s_copy(to, device):
        return pltpu.make_async_remote_copy(
            src_ref=ssend.at[to],
            dst_ref=srecv.at[h],
            send_sem=s_send.at[to],
            recv_sem=s_recv.at[h],
            device_id=device,
            device_id_type=MESH,
        )

    def landed(buffer, at, send_sem, recv_sem, frm):
        return pltpu.make_async_remote_copy(
            src_ref=buffer.at[at],
            dst_ref=buffer.at[at],
            send_sem=send_sem.at[frm],
            recv_sem=recv_sem.at[frm],
            device_id=sibling,
            device_id_type=MESH,
        )

    halos = []
    for way, device, plane in ((0, up, 7), (1, down, 0)):
        halos.append(
            pltpu.make_async_remote_copy(
                src_ref=markers.at[:, plane],
                dst_ref=mhalo.at[way],
                send_sem=h_send.at[2 * way],
                recv_sem=h_recv.at[2 * way],
                device_id=device,
                device_id_type=MESH,
            )
        )
        halos.append(
            pltpu.make_async_remote_copy(
                src_ref=velocity.at[plane],
                dst_ref=vhalo.at[way],
                send_sem=h_send.at[2 * way + 1],
                recv_sem=h_recv.at[2 * way + 1],
                device_id=device,
                device_id_type=MESH,
            )
        )

    def send_half(half):
        def send(i, _):
            to, device = target_in(half, i)
            x_copy(to, device).start()
            p_copy(to, device).start()
            return 0

        lax.fori_loop(0, jnp.where(parity == half, HALF - 1, HALF), send, 0)

    send_half(0)
    cut(1)
    send_half(1)
    for copy in halos:
        copy.start()
    x_all[c * CHIPS + h] = x_msg[...]
    pall[c * CHIPS + h] = ploc[h]

    def wait_x(j, _):
        frm = target(j)[0]
        landed(x_all, c * CHIPS + frm, x_send, x_recv, frm).wait_recv()
        return 0

    lax.fori_loop(0, CHIPS - 1, wait_x, 0)
    x_share = pltpu.make_async_remote_copy(
        src_ref=x_all.at[pl.ds(c * CHIPS, CHIPS)],
        dst_ref=x_all.at[pl.ds(c * CHIPS, CHIPS)],
        send_sem=xs_sem.at[0],
        recv_sem=xs_sem.at[1],
        device_id=sibling,
        device_id_type=MESH,
    )
    x_share.start()

    row = iota((256, LANES), 0)
    lane = iota((256, LANES), 1)
    from_peer = peer_at(row // 8, c)
    slot = lax.rem(row, 4)
    spread = []
    for s in range(2):
        hit = (lax.rem(slot, 2) == s) & (lane == from_peer + jnp.where(slot < 2, 0, BUB))
        spread.append(jnp.where(hit, 1.0, 0.0).astype(BF16))
    wanted = (lane - BUB * lax.rem(row // 4, 2)).astype(F32)

    row = iota((LANES, 256), 0)
    lane = iota((LANES, 256), 1)
    to_peer = peer_at(lax.rem(lane // 4, CHIPS), lane // LANES)
    slot = lax.rem(lane, 4)
    order = []
    for s in range(2):
        hit = (lax.rem(slot, 2) == s) & (row == to_peer + jnp.where(slot < 2, BUB, 0))
        order.append(jnp.where(hit, 1.0, 0.0).astype(BF16))

    x_share.wait()

    wide = jnp.zeros((256, 2 * CHIPS), F32)
    index = jnp.zeros((CHIPS, 256), F32)
    for s in range(2):
        wide += lax.dot_general(
            spread[s],
            x_all[:, s, :].astype(BF16),
            (((1,), (1,)), ((), ())),
            preferred_element_type=F32,
        )
        index += jnp.dot(
            x_all[pl.ds(c * CHIPS, CHIPS), s, :].astype(BF16),
            order[s],
            preferred_element_type=F32,
        )
    nidx[...] = index
    row = iota((256, 2 * CHIPS), 0)
    lane = iota((256, 2 * CHIPS), 1)
    wide = jnp.where(lax.rem(lane, 2) == lax.rem(row // 4, 2), wide, 0.0).astype(BF16)
    pair_of = iota((2 * CHIPS, LANES), 0) // 2

    def gather_matrix(k, _):
        pick = jnp.where(pair_of == k, 1.0, 0.0).astype(BF16)
        index = jnp.dot(wide, pick, preferred_element_type=F32)
        fbuf[k] = jnp.where(index == wanted, 1.0, 0.0).astype(BF16)
        return 0

    lax.fori_loop(0, PAIRS, gather_matrix, 0, unroll=2)

    bubble = iota((BUB, 2 * LANES), 0).astype(F32)

    def sum_matrix(q, _):
        nbuf[q] = jnp.where(bubble == nidx[pl.ds(q, 1), :], 1.0, 0.0).astype(BF16)
        return 0

    lax.fori_loop(0, CHIPS, sum_matrix, 0, unroll=4)

    def gather(line):
        for i in range(2):
            pair = 2 * line + i
            patches = pall[pl.ds(2 * pair, 2)].reshape(2 * BUB, LANES)
            partner = jnp.dot(fbuf[pair], patches, preferred_element_type=F32)
            g[:, pl.ds(pl.multiple_of(pair * 8, 8), 8), :] = partner.reshape(CHIPS, 8, LANES)

    def share(core, line):
        chips = pl.ds(core * CHIPS + line * 4, 4)
        return pltpu.make_async_remote_copy(
            src_ref=pall.at[chips],
            dst_ref=pall.at[chips],
            send_sem=ps_send.at[line],
            recv_sem=ps_recv.at[line],
            device_id=sibling,
            device_id_type=MESH,
        )

    def line_of(k):
        return (k // 4) * 4 + lax.rem(y // 2 + 2 + 3 * lax.rem(k, 4), 4)

    def own_line(k, _):
        line = line_of(k)

        def wait_p(i, _):
            frm = line * 4 + i

            @pl.when(frm != h)
            def _():
                landed(pall, c * CHIPS + frm, p_send, p_recv, frm).wait_recv()

            return 0

        lax.fori_loop(0, 4, wait_p, 0)
        share(c, line).start()
        gather(c * NY + line)
        return 0

    lax.fori_loop(0, NY, own_line, 0)

    def other_line(k, _):
        line = line_of(k)
        share(other, line).wait_recv()
        gather(other * NY + line)
        return 0

    lax.fori_loop(0, NY, other_line, 0)

    def sums(q):
        return jnp.dot(nbuf[q], g[q].astype(BF16), preferred_element_type=F32).astype(BF16)

    def send_s(j, _):
        to, device = target(j)
        ssend[to] = sums(to)
        s_copy(to, device).start()
        return 0

    lax.fori_loop(0, CHIPS - 1, send_s, 0)
    srecv[h] = sums(h)

    for copy in halos:
        copy.wait()
    low = jnp.where(gx == 0, 0.0, 1.0).astype(F32)
    high = jnp.where(gx == NZ - 1, 0.0, 1.0).astype(F32)

    def advect(t, _):
        rows = pl.ds(pl.multiple_of(t * 8, 8), 8)
        vel = [vhalo[0, rows, :] * low] + [velocity[i, rows, :] for i in range(8)]
        vel = vel + [vhalo[1, rows, :] * high]
        face = [0.5 * (vel[i] + vel[i + 1]) for i in range(9)]
        for m in range(4):
            mark = [mhalo[0, m, rows, :] * low] + [markers[m, i, rows, :] for i in range(8)]
            mark = mark + [mhalo[1, m, rows, :] * high]
            flux = [face[i] * jnp.where(face[i] > 0, mark[i], mark[i + 1]) for i in range(9)]
            for i in range(8):
                here = mark[i + 1]
                adv[m, i, rows, :] = (
                    here - (flux[i + 1] - flux[i]) + here * (face[i + 1] - face[i])
                )
        return 0

    lax.fori_loop(0, 8, advect, 0)

    def finish(at):
        patch = ploc[at].astype(F32)
        lanes = pl.ds(pl.multiple_of(at * LANES, LANES), LANES)
        force[:, lanes] = 0.8 * patch * (1.0 - patch) * srecv[at].astype(F32)

    finish(h)

    def wait_s(j, _):
        frm = target(j)[0]
        landed(srecv, frm, s_send, s_recv, frm).wait_recv()
        finish(frm)
        return 0

    lax.fori_loop(0, CHIPS - 1, wait_s, 0)

    def wait_sent(j, _):
        to, device = target(j)
        x_copy(to, device).wait_send()
        p_copy(to, device).wait_send()
        s_copy(to, device).wait_send()
        return 0

    lax.fori_loop(0, CHIPS - 1, wait_sent, 0)

    def wait_shared(line, _):
        share(c, line).wait_send()
        return 0

    lax.fori_loop(0, NY, wait_shared, 0)


def exchange(boxes, send_pick, recv_pick, count, markers, velocity):
    vmem = pl.BlockSpec(memory_space=pltpu.VMEM)
    hbm = pl.BlockSpec(memory_space=pltpu.HBM)
    dma = pltpu.SemaphoreType.DMA
    return pl.pallas_call(
        exchange_kernel,
        out_shape=(
            pltpu.VMEM(markers.shape, F32),
            pltpu.VMEM((BUB, CHIPS * LANES), F32),
        ),
        in_specs=[hbm] * 6,
        out_specs=[vmem] * 2,
        scratch_shapes=[
            pltpu.SMEM(boxes.shape, jnp.int32),
            pltpu.VMEM(send_pick.shape, jnp.int32),
            pltpu.VMEM(recv_pick.shape, jnp.int32),
            pltpu.VMEM(count.shape, jnp.int32),
            pltpu.VMEM(markers.shape, F32),
            pltpu.VMEM(velocity.shape, F32),
            pltpu.VMEM((BUB * HALF, LANES), F32),
            pltpu.VMEM((CHIPS, BUB, LANES), BF16),
            pltpu.VMEM((2, LANES), F32),
            pltpu.VMEM((2 * CHIPS, 2, LANES), F32),
            pltpu.VMEM((2 * CHIPS, BUB, LANES), BF16),
            pltpu.VMEM((PAIRS, 256, LANES), BF16),
            pltpu.VMEM((CHIPS, 256), F32),
            pltpu.VMEM((CHIPS, BUB, 2 * LANES), BF16),
            pltpu.VMEM((CHIPS, 256, LANES), F32),
            pltpu.VMEM((CHIPS, BUB, LANES), BF16),
            pltpu.VMEM((CHIPS, BUB, LANES), BF16),
            pltpu.VMEM((2, 4, 64, LANES), F32),
            pltpu.VMEM((2, 64, LANES), F32),
            dma((9,)),
            dma((CHIPS,)),
            dma((CHIPS,)),
            dma((2,)),
            dma((CHIPS,)),
            dma((CHIPS,)),
            dma((NY,)),
            dma((NY,)),
            dma((CHIPS,)),
            dma((CHIPS,)),
            dma((4,)),
            dma((4,)),
        ],
        compiler_params=pltpu.CompilerParams(
            collective_id=0, has_side_effects=True, vmem_limit_bytes=60 * 1024 * 1024
        ),
    )(boxes, send_pick, recv_pick, count, markers, velocity)


def write_kernel(adv, force, adv_out, force_out, sem):
    copies = []
    for i in range(4):
        copies.append(pltpu.make_async_copy(adv.at[i], adv_out.at[i], sem.at[i]))
        part = pl.ds(16 * i, 16)
        copies.append(pltpu.make_async_copy(force.at[part], force_out.at[part], sem.at[4 + i]))
    for copy in copies:
        copy.start()
    for copy in copies:
        copy.wait()


def write(adv, force):
    return pl.pallas_call(
        write_kernel,
        out_shape=(
            jax.ShapeDtypeStruct(adv.shape, F32),
            jax.ShapeDtypeStruct(force.shape, F32),
        ),
        in_specs=[pl.BlockSpec(memory_space=pltpu.VMEM)] * 2,
        out_specs=[pl.BlockSpec(memory_space=pl.ANY)] * 2,
        scratch_shapes=[pltpu.SemaphoreType.DMA((8,))],
        compiler_params=pltpu.CompilerParams(vmem_limit_bytes=16 * 1024 * 1024),
    )(adv, force)


def on_device(markers, velocity, patch_boxes, send_pick, recv_pick, pair_count):
    peers, slots = send_pick.shape[-2:]
    adv, force = exchange(
        patch_boxes,
        send_pick.reshape(peers, slots).T,
        recv_pick.reshape(peers, slots).T,
        pair_count.reshape(1, peers),
        markers,
        velocity,
    )
    return tuple(write(adv, force))


def solution(mesh):
    placed = (
        P(None, "gx", "gy", "gz"),
        P("gx", "gy", "gz"),
        P(None, ("gx", "gy", "gz")),
        P("gx", "gy", "gz", None, None),
        P("gx", "gy", "gz", None, None),
        P("gx", "gy", "gz", None),
    )
    return jax.shard_map(
        on_device,
        mesh=mesh,
        in_specs=placed,
        out_specs=(P(None, "gx", "gy", "gz"), P(("gx", "gy", "gz"), None)),
        check_vma=False,
    )
```

```python
import jax
import jax.numpy as jnp
from jax import lax
from jax.experimental import pallas as pl
from jax.experimental.pallas import tpu as pltpu
from jax.sharding import PartitionSpec as P

MESH = pl.DeviceIdType.MESH
PATCH = 32
BUB = 64
NY = 8
NX = 4
NZ = 12
CHIPS = NX * NY
HALF = CHIPS // 2
PAIRS = CHIPS
LANES = 128
UNUSED = 512.0
ROWS = (4, 3, 5, 2, 6, 1, 7, 0)
F32 = jnp.float32
BF16 = jnp.bfloat16


def iota(shape, dim):
    return lax.broadcasted_iota(jnp.int32, shape, dim)


def chip_at(h):
    y = lax.rem(h, HALF) // 2
    return 2 * lax.rem(h, 2) + lax.rem(h // HALF + y, 2), y


def peer_at(h, core):
    gy, y = chip_at(h)
    return gy * 16 + y * 2 + core


def exchange_kernel(
    boxes_hbm,
    send_hbm,
    recv_hbm,
    count_hbm,
    markers_hbm,
    velocity_hbm,
    adv,
    force,
    boxes,
    send_pick,
    recv_pick,
    count,
    markers,
    velocity,
    tmp,
    ploc,
    x_msg,
    x_all,
    pall,
    fbuf,
    nidx,
    nbuf,
    g,
    ssend,
    srecv,
    mhalo,
    vhalo,
    in_sem,
    x_send,
    x_recv,
    xs_sem,
    p_send,
    p_recv,
    ps_send,
    ps_recv,
    s_send,
    s_recv,
    h_send,
    h_recv,
):
    gx = lax.axis_index("gx")
    gy = lax.axis_index("gy")
    gz = lax.axis_index("gz")
    y = gz // 2
    c = lax.rem(gz, 2)
    parity = lax.rem(gy + y, 2)
    h = parity * HALF + y * 2 + gy // 2
    other = 1 - c
    sibling = (gx, gy, y * 2 + other)
    up = (lax.rem(gx + 1, NZ), gy, gz)
    down = (lax.rem(gx + NZ - 1, NZ), gy, gz)

    loads = []
    for src, dst in (
        (boxes_hbm, boxes),
        (send_hbm, send_pick),
        (recv_hbm, recv_pick),
        (count_hbm, count),
        *((markers_hbm.at[m], markers.at[m]) for m in range(4)),
        (velocity_hbm, velocity),
    ):
        loads.append(pltpu.make_async_copy(src, dst, in_sem.at[len(loads)]))
        loads[-1].start()

    ys = [lax.rem(y + dy, NY) for dy in range(NY)]
    xs = [lax.rem(gy + dx, NX) for dx in range(NX)]
    base = [[lax.rem(parity + i, 2) * HALF + xs[dx] // 2 for dx in range(NX)] for i in range(2)]

    def place(dx, dy):
        number = base[(dx + dy) % 2][dx] + ys[dy] * 2
        return number, (gx, xs[dx], ys[dy] * 2 + c)

    others = [place(dx, dy) for dy in ROWS for dx in (1, 2, 3, 0)][:-1]

    def others_in(half):
        same = parity == half
        even = [jnp.where(same, xs[dx], xs[dx + 1]) for dx in (2, 0)]
        odd = [jnp.where(same, xs[dx + 1], xs[dx]) for dx in (2, 0)]
        found = []
        for dy in ROWS:
            for at in odd if dy % 2 else even:
                found.append((half * HALF + ys[dy] * 2 + at // 2, (gx, at, ys[dy] * 2 + c)))
        return found

    def row_of(k):
        m = 4 - (k + 1) // 2
        ty = lax.rem(y + m + (1 - lax.rem(k, 2)) * (8 - 2 * m), NY)
        odd = lax.rem(ty - y + NY, 2)
        row = []
        for dx in (1, 2, 3, 0):
            at = lax.rem(parity + odd + dx, 2) * HALF + ty * 2 + xs[dx] // 2
            row.append((at, (gx, xs[dx], ty * 2 + c)))
        return row

    barrier = pltpu.get_barrier_semaphore()

    for _, device in others:
        pl.semaphore_signal(barrier, inc=1, device_id=device, device_id_type=MESH)
    for device in (sibling, up, down):
        pl.semaphore_signal(barrier, inc=1, device_id=device, device_id_type=MESH)

    for copy in loads:
        copy.wait()

    for s in range(2):
        far = jnp.where(count[...] > s, send_pick[s : s + 1, :].astype(F32), UNUSED)
        x_msg[s : s + 1, 0:BUB] = far
        x_msg[s : s + 1, BUB:LANES] = recv_pick[s : s + 1, :].astype(F32)

    group = iota((8, LANES), 1) // PATCH
    rows = markers.reshape(4 * 8 * 64, LANES)

    def cut(half):
        def one(b, _):
            base = (boxes[0, b] * 8 + boxes[1, b]) * 64 + boxes[2, b]
            z0 = boxes[3, b]
            for dx in range(2):
                cells = None
                for j in range(4):
                    piece = rows[pl.ds(base + (2 * half + dx) * 64 + j, 8, stride=4), :]
                    piece = pltpu.roll(piece, lax.rem(PATCH * j - z0 + LANES, LANES), 1)
                    cells = piece if j == 0 else jnp.where(group == j, piece, cells)
                tmp[pl.ds(pl.multiple_of(b * HALF + dx * 8, 8), 8), :] = cells
            return 0

        lax.fori_loop(0, BUB, one, 0, unroll=8)

        def put(s, _):
            ploc[half * HALF + s] = tmp[pl.ds(s, BUB, stride=HALF), :].astype(BF16)
            return 0

        lax.fori_loop(0, HALF, put, 0, unroll=4)

    cut(0)

    pl.semaphore_wait(barrier, CHIPS - 1 + 3)

    def x_copy(to, device):
        return pltpu.make_async_remote_copy(
            src_ref=x_msg,
            dst_ref=x_all.at[c * CHIPS + h],
            send_sem=x_send.at[to],
            recv_sem=x_recv.at[h],
            device_id=device,
            device_id_type=MESH,
        )

    def p_copy(to, device):
        return pltpu.make_async_remote_copy(
            src_ref=ploc.at[to],
            dst_ref=pall.at[c * CHIPS + h],
            send_sem=p_send.at[to],
            recv_sem=p_recv.at[h],
            device_id=device,
            device_id_type=MESH,
        )

    def s_copy(to, device):
        return pltpu.make_async_remote_copy(
            src_ref=ssend.at[to],
            dst_ref=srecv.at[h],
            send_sem=s_send.at[to],
            recv_sem=s_recv.at[h],
            device_id=device,
            device_id_type=MESH,
        )

    def landed(buffer, at, send_sem, recv_sem, frm):
        return pltpu.make_async_remote_copy(
            src_ref=buffer.at[at],
            dst_ref=buffer.at[at],
            send_sem=send_sem.at[frm],
            recv_sem=recv_sem.at[frm],
            device_id=sibling,
            device_id_type=MESH,
        )

    halos = []
    for way, device, plane in ((0, up, 7), (1, down, 0)):
        halos.append(
            pltpu.make_async_remote_copy(
                src_ref=markers.at[:, plane],
                dst_ref=mhalo.at[way],
                send_sem=h_send.at[2 * way],
                recv_sem=h_recv.at[2 * way],
                device_id=device,
                device_id_type=MESH,
            )
        )
        halos.append(
            pltpu.make_async_remote_copy(
                src_ref=velocity.at[plane],
                dst_ref=vhalo.at[way],
                send_sem=h_send.at[2 * way + 1],
                recv_sem=h_recv.at[2 * way + 1],
                device_id=device,
                device_id_type=MESH,
            )
        )

    def send_half(half):
        found = others_in(half)
        for to, device in found[:-1]:
            p_copy(to, device).start()

        @pl.when(parity != half)
        def _():
            p_copy(*found[-1]).start()

    for to, device in others:
        x_copy(to, device).start()
    send_half(0)
    cut(1)
    send_half(1)
    for copy in halos:
        copy.start()
    x_all[c * CHIPS + h] = x_msg[...]
    pall[c * CHIPS + h] = ploc[h]

    for frm, _ in others:
        landed(x_all, c * CHIPS + frm, x_send, x_recv, frm).wait_recv()
    x_share = pltpu.make_async_remote_copy(
        src_ref=x_all.at[pl.ds(c * CHIPS, CHIPS)],
        dst_ref=x_all.at[pl.ds(c * CHIPS, CHIPS)],
        send_sem=xs_sem.at[0],
        recv_sem=xs_sem.at[1],
        device_id=sibling,
        device_id_type=MESH,
    )
    x_share.start()

    row = iota((256, LANES), 0)
    lane = iota((256, LANES), 1)
    from_peer = peer_at(row // 8, c)
    slot = lax.rem(row, 4)
    spread = []
    for s in range(2):
        hit = (lax.rem(slot, 2) == s) & (lane == from_peer + jnp.where(slot < 2, 0, BUB))
        spread.append(jnp.where(hit, 1.0, 0.0).astype(BF16))
    wanted = (lane - BUB * lax.rem(row // 4, 2)).astype(F32)

    row = iota((LANES, 256), 0)
    lane = iota((LANES, 256), 1)
    to_peer = peer_at(lax.rem(lane // 4, CHIPS), lane // LANES)
    slot = lax.rem(lane, 4)
    order = []
    for s in range(2):
        hit = (lax.rem(slot, 2) == s) & (row == to_peer + jnp.where(slot < 2, BUB, 0))
        order.append(jnp.where(hit, 1.0, 0.0).astype(BF16))

    half_row = iota((256, CHIPS), 0)
    half_lane = iota((256, CHIPS), 1)
    pair_half = lax.rem(half_lane, 2) == lax.rem(half_row // 4, 2)
    pair_of = iota((CHIPS, LANES), 0) // 2

    def gather_matrices(core):
        wide = jnp.zeros((256, CHIPS), F32)
        for s in range(2):
            wide += lax.dot_general(
                spread[s],
                x_all[pl.ds(core * CHIPS, CHIPS), s, :].astype(BF16),
                (((1,), (1,)), ((), ())),
                preferred_element_type=F32,
            )
        wide = jnp.where(pair_half, wide, 0.0).astype(BF16)

        def matrix(k, _):
            pick = jnp.where(pair_of == k, 1.0, 0.0).astype(BF16)
            index = jnp.dot(wide, pick, preferred_element_type=F32)
            fbuf[core * HALF + k] = jnp.where(index == wanted, 1.0, 0.0).astype(BF16)
            return 0

        lax.fori_loop(0, HALF, matrix, 0, unroll=8)

    gather_matrices(c)

    index = jnp.zeros((CHIPS, 256), F32)
    for s in range(2):
        index += jnp.dot(
            x_all[pl.ds(c * CHIPS, CHIPS), s, :].astype(BF16),
            order[s],
            preferred_element_type=F32,
        )
    nidx[...] = index
    bubble = iota((BUB, 2 * LANES), 0).astype(F32)

    def sum_matrix(q, _):
        nbuf[q] = jnp.where(bubble == nidx[pl.ds(q, 1), :], 1.0, 0.0).astype(BF16)
        return 0

    lax.fori_loop(0, CHIPS, sum_matrix, 0, unroll=4)

    def gather(core, half):
        for i in range(8):
            pair = core * HALF + half * 8 + i
            patches = pall[pl.ds(2 * pair, 2)].reshape(2 * BUB, LANES)
            partner = jnp.dot(fbuf[pair], patches, preferred_element_type=F32)
            g[:, pl.ds(pl.multiple_of(pair * 8, 8), 8), :] = partner.reshape(CHIPS, 8, LANES)

    def share(core, line):
        chips = pl.ds(core * CHIPS + line * 4, 4)
        return pltpu.make_async_remote_copy(
            src_ref=pall.at[chips],
            dst_ref=pall.at[chips],
            send_sem=ps_send.at[line],
            recv_sem=ps_recv.at[line],
            device_id=sibling,
            device_id_type=MESH,
        )

    def lines(half):
        return [half * 4 + lax.rem(y // 2 + step, 4) for step in (2, 1, 3, 0)]

    for half in range(2):
        for line in lines(half):
            for i in range(4):
                frm = line * 4 + i

                @pl.when(frm != h)
                def _():
                    landed(pall, c * CHIPS + frm, p_send, p_recv, frm).wait_recv()

            share(c, line).start()
        gather(c, half)

    x_share.wait()
    gather_matrices(other)

    for half in range(2):
        for line in lines(half):
            share(other, line).wait_recv()
        gather(other, half)

    def send_s(k, _):
        row = row_of(k)
        for to, _ in row:
            part = jnp.dot(nbuf[to], g[to].astype(BF16), preferred_element_type=F32)
            ssend[to] = part.astype(BF16)
        for to, device in row[:-1]:
            s_copy(to, device).start()

        @pl.when(k < NY - 1)
        def _():
            s_copy(*row[-1]).start()

        return 0

    lax.fori_loop(0, NY, send_s, 0)
    srecv[h] = ssend[h]

    for to, device in others:
        x_copy(to, device).wait_send()
        p_copy(to, device).wait_send()
    for line in range(NY):
        share(c, line).wait_send()

    for copy in halos:
        copy.wait()
    low = jnp.where(gx == 0, 0.0, 1.0).astype(F32)
    high = jnp.where(gx == NZ - 1, 0.0, 1.0).astype(F32)

    def advect(t, _):
        rows = pl.ds(pl.multiple_of(t * 8, 8), 8)
        vel = [vhalo[0, rows, :] * low] + [velocity[i, rows, :] for i in range(8)]
        vel = vel + [vhalo[1, rows, :] * high]
        face = [0.5 * (vel[i] + vel[i + 1]) for i in range(9)]
        for m in range(4):
            mark = [mhalo[0, m, rows, :] * low] + [markers[m, i, rows, :] for i in range(8)]
            mark = mark + [mhalo[1, m, rows, :] * high]
            flux = [face[i] * jnp.where(face[i] > 0, mark[i], mark[i + 1]) for i in range(9)]
            for i in range(8):
                here = mark[i + 1]
                adv[m, i, rows, :] = (
                    here - (flux[i + 1] - flux[i]) + here * (face[i + 1] - face[i])
                )
        return 0

    lax.fori_loop(0, 8, advect, 0)

    def finish(at):
        patch = ploc[at].astype(F32)
        lanes = pl.ds(pl.multiple_of(at * LANES, LANES), LANES)
        force[:, lanes] = 0.8 * patch * (1.0 - patch) * srecv[at].astype(F32)

    def finish_row(k, _):
        row = row_of(k)
        for at, device in row[:-1]:
            landed(srecv, at, s_send, s_recv, at).wait_recv()
            s_copy(at, device).wait_send()

        @pl.when(k < NY - 1)
        def _():
            at, device = row[-1]
            landed(srecv, at, s_send, s_recv, at).wait_recv()
            s_copy(at, device).wait_send()

        for at, _ in row:
            finish(at)
        return 0

    lax.fori_loop(0, NY, finish_row, 0)


def exchange(boxes, send_pick, recv_pick, count, markers, velocity):
    vmem = pl.BlockSpec(memory_space=pltpu.VMEM)
    hbm = pl.BlockSpec(memory_space=pltpu.HBM)
    dma = pltpu.SemaphoreType.DMA
    return pl.pallas_call(
        exchange_kernel,
        out_shape=(
            pltpu.VMEM(markers.shape, F32),
            pltpu.VMEM((BUB, CHIPS * LANES), F32),
        ),
        in_specs=[hbm] * 6,
        out_specs=[vmem] * 2,
        scratch_shapes=[
            pltpu.SMEM(boxes.shape, jnp.int32),
            pltpu.VMEM(send_pick.shape, jnp.int32),
            pltpu.VMEM(recv_pick.shape, jnp.int32),
            pltpu.VMEM(count.shape, jnp.int32),
            pltpu.VMEM(markers.shape, F32),
            pltpu.VMEM(velocity.shape, F32),
            pltpu.VMEM((BUB * HALF, LANES), F32),
            pltpu.VMEM((CHIPS, BUB, LANES), BF16),
            pltpu.VMEM((2, LANES), F32),
            pltpu.VMEM((2 * CHIPS, 2, LANES), F32),
            pltpu.VMEM((2 * CHIPS, BUB, LANES), BF16),
            pltpu.VMEM((PAIRS, 256, LANES), BF16),
            pltpu.VMEM((CHIPS, 256), F32),
            pltpu.VMEM((CHIPS, BUB, 2 * LANES), BF16),
            pltpu.VMEM((CHIPS, 256, LANES), F32),
            pltpu.VMEM((CHIPS, BUB, LANES), BF16),
            pltpu.VMEM((CHIPS, BUB, LANES), BF16),
            pltpu.VMEM((2, 4, 64, LANES), F32),
            pltpu.VMEM((2, 64, LANES), F32),
            dma((9,)),
            dma((CHIPS,)),
            dma((CHIPS,)),
            dma((2,)),
            dma((CHIPS,)),
            dma((CHIPS,)),
            dma((NY,)),
            dma((NY,)),
            dma((CHIPS,)),
            dma((CHIPS,)),
            dma((4,)),
            dma((4,)),
        ],
        compiler_params=pltpu.CompilerParams(
            collective_id=0, has_side_effects=True, vmem_limit_bytes=60 * 1024 * 1024
        ),
    )(boxes, send_pick, recv_pick, count, markers, velocity)


def write_kernel(adv, force, adv_out, force_out, sem):
    copies = []
    for i in range(4):
        copies.append(pltpu.make_async_copy(adv.at[i], adv_out.at[i], sem.at[i]))
        part = pl.ds(16 * i, 16)
        copies.append(pltpu.make_async_copy(force.at[part], force_out.at[part], sem.at[4 + i]))
    for copy in copies:
        copy.start()
    for copy in copies:
        copy.wait()


def write(adv, force):
    return pl.pallas_call(
        write_kernel,
        out_shape=(
            jax.ShapeDtypeStruct(adv.shape, F32),
            jax.ShapeDtypeStruct(force.shape, F32),
        ),
        in_specs=[pl.BlockSpec(memory_space=pltpu.VMEM)] * 2,
        out_specs=[pl.BlockSpec(memory_space=pl.ANY)] * 2,
        scratch_shapes=[pltpu.SemaphoreType.DMA((8,))],
        compiler_params=pltpu.CompilerParams(vmem_limit_bytes=16 * 1024 * 1024),
    )(adv, force)


def on_device(markers, velocity, patch_boxes, send_pick, recv_pick, pair_count):
    peers, slots = send_pick.shape[-2:]
    adv, force = exchange(
        patch_boxes,
        send_pick.reshape(peers, slots).T,
        recv_pick.reshape(peers, slots).T,
        pair_count.reshape(1, peers),
        markers,
        velocity,
    )
    return tuple(write(adv, force))


def solution(mesh):
    placed = (
        P(None, "gx", "gy", "gz"),
        P("gx", "gy", "gz"),
        P(None, ("gx", "gy", "gz")),
        P("gx", "gy", "gz", None, None),
        P("gx", "gy", "gz", None, None),
        P("gx", "gy", "gz", None),
    )
    return jax.shard_map(
        on_device,
        mesh=mesh,
        in_specs=placed,
        out_specs=(P(None, "gx", "gy", "gz"), P(("gx", "gy", "gz"), None)),
        check_vma=False,
    )
```

```python
import jax
import jax.numpy as jnp
from jax import lax
from jax.experimental import pallas as pl
from jax.experimental.pallas import tpu as pltpu
from jax.sharding import PartitionSpec as P

MESH = pl.DeviceIdType.MESH
PATCH = 32
BUB = 64
NY = 8
NX = 4
NZ = 12
CHIPS = NX * NY
HALF = CHIPS // 2
PAIRS = CHIPS
LANES = 128
UNUSED = 512.0
ROWS = (4, 3, 5, 2, 6, 1, 7, 0)
F32 = jnp.float32
BF16 = jnp.bfloat16


def iota(shape, dim):
    return lax.broadcasted_iota(jnp.int32, shape, dim)


def chip_at(h):
    y = lax.rem(h, HALF) // 2
    return 2 * lax.rem(h, 2) + lax.rem(h // HALF + y, 2), y


def peer_at(h, core):
    gy, y = chip_at(h)
    return gy * 16 + y * 2 + core


def exchange_kernel(
    boxes_hbm,
    send_hbm,
    recv_hbm,
    count_hbm,
    markers_hbm,
    velocity_hbm,
    adv,
    force,
    boxes,
    send_pick,
    recv_pick,
    count,
    markers,
    velocity,
    tmp,
    ploc,
    x_msg,
    x_all,
    pall,
    fbuf,
    nidx,
    nbuf,
    g,
    ssend,
    srecv,
    mhalo,
    vhalo,
    in_sem,
    x_send,
    x_recv,
    xs_sem,
    p_send,
    p_recv,
    ps_send,
    ps_recv,
    s_send,
    s_recv,
    h_send,
    h_recv,
):
    gx = lax.axis_index("gx")
    gy = lax.axis_index("gy")
    gz = lax.axis_index("gz")
    y = gz // 2
    c = lax.rem(gz, 2)
    parity = lax.rem(gy + y, 2)
    h = parity * HALF + y * 2 + gy // 2
    other = 1 - c
    sibling = (gx, gy, y * 2 + other)
    sides = ((gx < NZ - 1, (gx + 1, gy, gz), 7), (gx > 0, (gx - 1, gy, gz), 0))

    loads = []
    for src, dst in (
        (boxes_hbm, boxes),
        (send_hbm, send_pick),
        (recv_hbm, recv_pick),
        (count_hbm, count),
        *((markers_hbm.at[m], markers.at[m]) for m in range(4)),
        (velocity_hbm, velocity),
    ):
        loads.append(pltpu.make_async_copy(src, dst, in_sem.at[len(loads)]))
        loads[-1].start()

    ys = [lax.rem(y + dy, NY) for dy in range(NY)]
    xs = [lax.rem(gy + dx, NX) for dx in range(NX)]
    base = [[lax.rem(parity + i, 2) * HALF + xs[dx] // 2 for dx in range(NX)] for i in range(2)]

    def place(dx, dy):
        number = base[(dx + dy) % 2][dx] + ys[dy] * 2
        return number, (gx, xs[dx], ys[dy] * 2 + c)

    others = [place(dx, dy) for dy in ROWS for dx in (1, 2, 3, 0)][:-1]

    def others_in(half):
        same = parity == half
        even = [jnp.where(same, xs[dx], xs[dx + 1]) for dx in (2, 0)]
        odd = [jnp.where(same, xs[dx + 1], xs[dx]) for dx in (2, 0)]
        found = []
        for dy in ROWS:
            for at in odd if dy % 2 else even:
                found.append((half * HALF + ys[dy] * 2 + at // 2, (gx, at, ys[dy] * 2 + c)))
        return found

    def row_of(k):
        m = 4 - (k + 1) // 2
        ty = lax.rem(y + m + (1 - lax.rem(k, 2)) * (8 - 2 * m), NY)
        odd = lax.rem(ty - y + NY, 2)
        row = []
        for dx in (1, 2, 3, 0):
            at = lax.rem(parity + odd + dx, 2) * HALF + ty * 2 + xs[dx] // 2
            row.append((at, (gx, xs[dx], ty * 2 + c)))
        return row

    barrier = pltpu.get_barrier_semaphore()

    for _, device in others:
        pl.semaphore_signal(barrier, inc=1, device_id=device, device_id_type=MESH)
    pl.semaphore_signal(barrier, inc=1, device_id=sibling, device_id_type=MESH)
    for there, device, _ in sides:

        @pl.when(there)
        def _():
            pl.semaphore_signal(barrier, inc=1, device_id=device, device_id_type=MESH)


    for copy in loads:
        copy.wait()

    for s in range(2):
        far = jnp.where(count[...] > s, send_pick[s : s + 1, :].astype(F32), UNUSED)
        x_msg[s : s + 1, 0:BUB] = far
        x_msg[s : s + 1, BUB:LANES] = recv_pick[s : s + 1, :].astype(F32)

    group = iota((8, LANES), 1) // PATCH
    rows = markers.reshape(4 * 8 * 64, LANES)

    def cut(half):
        def one(b, _):
            base = (boxes[0, b] * 8 + boxes[1, b]) * 64 + boxes[2, b]
            z0 = boxes[3, b]
            for dx in range(2):
                cells = None
                for j in range(4):
                    piece = rows[pl.ds(base + (2 * half + dx) * 64 + j, 8, stride=4), :]
                    piece = pltpu.roll(piece, lax.rem(PATCH * j - z0 + LANES, LANES), 1)
                    cells = piece if j == 0 else jnp.where(group == j, piece, cells)
                tmp[pl.ds(pl.multiple_of(b * HALF + dx * 8, 8), 8), :] = cells
            return 0

        lax.fori_loop(0, BUB, one, 0, unroll=8)

        def put(s, _):
            ploc[half * HALF + s] = tmp[pl.ds(s, BUB, stride=HALF), :].astype(BF16)
            return 0

        lax.fori_loop(0, HALF, put, 0, unroll=4)

    cut(0)

    neighbours = jnp.where(gx < NZ - 1, 1, 0) + jnp.where(gx > 0, 1, 0)
    pl.semaphore_wait(barrier, CHIPS + neighbours)

    def x_copy(to, device):
        return pltpu.make_async_remote_copy(
            src_ref=x_msg,
            dst_ref=x_all.at[c * CHIPS + h],
            send_sem=x_send.at[to],
            recv_sem=x_recv.at[h],
            device_id=device,
            device_id_type=MESH,
        )

    def p_copy(to, device):
        return pltpu.make_async_remote_copy(
            src_ref=ploc.at[to],
            dst_ref=pall.at[c * CHIPS + h],
            send_sem=p_send.at[to],
            recv_sem=p_recv.at[h],
            device_id=device,
            device_id_type=MESH,
        )

    def s_copy(to, device):
        return pltpu.make_async_remote_copy(
            src_ref=ssend.at[to],
            dst_ref=srecv.at[h],
            send_sem=s_send.at[to],
            recv_sem=s_recv.at[h],
            device_id=device,
            device_id_type=MESH,
        )

    def landed(buffer, at, send_sem, recv_sem, frm):
        return pltpu.make_async_remote_copy(
            src_ref=buffer.at[at],
            dst_ref=buffer.at[at],
            send_sem=send_sem.at[frm],
            recv_sem=recv_sem.at[frm],
            device_id=sibling,
            device_id_type=MESH,
        )

    def halo_copies(way):
        _, device, plane = sides[way]
        return (
            pltpu.make_async_remote_copy(
                src_ref=markers.at[:, plane],
                dst_ref=mhalo.at[way],
                send_sem=h_send.at[2 * way],
                recv_sem=h_recv.at[2 * way],
                device_id=device,
                device_id_type=MESH,
            ),
            pltpu.make_async_remote_copy(
                src_ref=velocity.at[plane],
                dst_ref=vhalo.at[way],
                send_sem=h_send.at[2 * way + 1],
                recv_sem=h_recv.at[2 * way + 1],
                device_id=device,
                device_id_type=MESH,
            ),
        )

    def send_half(half):
        found = others_in(half)
        for to, device in found[:-1]:
            p_copy(to, device).start()

        @pl.when(parity != half)
        def _():
            p_copy(*found[-1]).start()

    for to, device in others:
        x_copy(to, device).start()
    send_half(0)
    cut(1)
    send_half(1)
    for way in range(2):

        @pl.when(sides[way][0])
        def _():
            for copy in halo_copies(way):
                copy.start()

    x_all[c * CHIPS + h] = x_msg[...]
    pall[c * CHIPS + h] = ploc[h]

    for frm, _ in others:
        landed(x_all, c * CHIPS + frm, x_send, x_recv, frm).wait_recv()
    x_share = pltpu.make_async_remote_copy(
        src_ref=x_all.at[pl.ds(c * CHIPS, CHIPS)],
        dst_ref=x_all.at[pl.ds(c * CHIPS, CHIPS)],
        send_sem=xs_sem.at[0],
        recv_sem=xs_sem.at[1],
        device_id=sibling,
        device_id_type=MESH,
    )
    x_share.start()

    row = iota((256, LANES), 0)
    lane = iota((256, LANES), 1)
    from_peer = peer_at(row // 8, c)
    slot = lax.rem(row, 4)
    spread = []
    for s in range(2):
        hit = (lax.rem(slot, 2) == s) & (lane == from_peer + jnp.where(slot < 2, 0, BUB))
        spread.append(jnp.where(hit, 1.0, 0.0).astype(BF16))
    wanted = (lane - BUB * lax.rem(row // 4, 2)).astype(F32)

    row = iota((LANES, 256), 0)
    lane = iota((LANES, 256), 1)
    to_peer = peer_at(lax.rem(lane // 4, CHIPS), lane // LANES)
    slot = lax.rem(lane, 4)
    order = []
    for s in range(2):
        hit = (lax.rem(slot, 2) == s) & (row == to_peer + jnp.where(slot < 2, BUB, 0))
        order.append(jnp.where(hit, 1.0, 0.0).astype(BF16))

    half_row = iota((256, CHIPS), 0)
    half_lane = iota((256, CHIPS), 1)
    pair_half = lax.rem(half_lane, 2) == lax.rem(half_row // 4, 2)
    pair_of = iota((CHIPS, LANES), 0) // 2

    def gather_matrices(core):
        wide = jnp.zeros((256, CHIPS), F32)
        for s in range(2):
            wide += lax.dot_general(
                spread[s],
                x_all[pl.ds(core * CHIPS, CHIPS), s, :].astype(BF16),
                (((1,), (1,)), ((), ())),
                preferred_element_type=F32,
            )
        wide = jnp.where(pair_half, wide, 0.0).astype(BF16)

        def matrix(k, _):
            pick = jnp.where(pair_of == k, 1.0, 0.0).astype(BF16)
            index = jnp.dot(wide, pick, preferred_element_type=F32)
            fbuf[core * HALF + k] = jnp.where(index == wanted, 1.0, 0.0).astype(BF16)
            return 0

        lax.fori_loop(0, HALF, matrix, 0, unroll=8)

    gather_matrices(c)

    index = jnp.zeros((CHIPS, 256), F32)
    for s in range(2):
        index += jnp.dot(
            x_all[pl.ds(c * CHIPS, CHIPS), s, :].astype(BF16),
            order[s],
            preferred_element_type=F32,
        )
    nidx[...] = index
    bubble = iota((BUB, 2 * LANES), 0).astype(F32)

    def sum_matrix(q, _):
        nbuf[q] = jnp.where(bubble == nidx[pl.ds(q, 1), :], 1.0, 0.0).astype(BF16)
        return 0

    lax.fori_loop(0, CHIPS, sum_matrix, 0, unroll=4)

    def gather(core, half):
        for i in range(8):
            pair = core * HALF + half * 8 + i
            patches = pall[pl.ds(2 * pair, 2)].reshape(2 * BUB, LANES)
            partner = jnp.dot(fbuf[pair], patches, preferred_element_type=F32)
            g[:, pl.ds(pl.multiple_of(pair * 8, 8), 8), :] = partner.reshape(CHIPS, 8, LANES)

    def share(core, line):
        chips = pl.ds(core * CHIPS + line * 4, 4)
        return pltpu.make_async_remote_copy(
            src_ref=pall.at[chips],
            dst_ref=pall.at[chips],
            send_sem=ps_send.at[line],
            recv_sem=ps_recv.at[line],
            device_id=sibling,
            device_id_type=MESH,
        )

    def lines(half):
        return [half * 4 + lax.rem(y // 2 + step, 4) for step in (2, 1, 3, 0)]

    for half in range(2):
        for line in lines(half):
            for i in range(4):
                frm = line * 4 + i

                @pl.when(frm != h)
                def _():
                    landed(pall, c * CHIPS + frm, p_send, p_recv, frm).wait_recv()

            share(c, line).start()
        gather(c, half)

    x_share.wait()
    gather_matrices(other)

    for half in range(2):
        for line in lines(half):
            share(other, line).wait_recv()
        gather(other, half)

    def send_s(k, _):
        row = row_of(k)
        for to, _ in row:
            part = jnp.dot(nbuf[to], g[to].astype(BF16), preferred_element_type=F32)
            ssend[to] = part.astype(BF16)
        for to, device in row[:-1]:
            s_copy(to, device).start()

        @pl.when(k < NY - 1)
        def _():
            s_copy(*row[-1]).start()

        return 0

    lax.fori_loop(0, NY, send_s, 0)
    srecv[h] = ssend[h]

    for to, device in others:
        x_copy(to, device).wait_send()
        p_copy(to, device).wait_send()
    for line in range(NY):
        share(c, line).wait_send()

    for way in range(2):

        @pl.when(sides[way][0])
        def _():
            for copy in halo_copies(way):
                copy.wait_send()

        @pl.when(sides[1 - way][0])
        def _():
            for copy in halo_copies(way):
                copy.wait_recv()

        @pl.when(jnp.logical_not(sides[1 - way][0]))
        def _():
            mhalo[way] = jnp.zeros(mhalo.shape[1:], F32)
            vhalo[way] = jnp.zeros(vhalo.shape[1:], F32)


    def advect(t, _):
        rows = pl.ds(pl.multiple_of(t * 8, 8), 8)
        vel = [vhalo[0, rows, :]] + [velocity[i, rows, :] for i in range(8)]
        vel = vel + [vhalo[1, rows, :]]
        face = [0.5 * (vel[i] + vel[i + 1]) for i in range(9)]
        for m in range(4):
            mark = [mhalo[0, m, rows, :]] + [markers[m, i, rows, :] for i in range(8)]
            mark = mark + [mhalo[1, m, rows, :]]
            flux = [face[i] * jnp.where(face[i] > 0, mark[i], mark[i + 1]) for i in range(9)]
            for i in range(8):
                here = mark[i + 1]
                adv[m, i, rows, :] = (
                    here - (flux[i + 1] - flux[i]) + here * (face[i + 1] - face[i])
                )
        return 0

    lax.fori_loop(0, 8, advect, 0)

    def finish(at):
        patch = ploc[at].astype(F32)
        lanes = pl.ds(pl.multiple_of(at * LANES, LANES), LANES)
        force[:, lanes] = 0.8 * patch * (1.0 - patch) * srecv[at].astype(F32)

    def finish_row(k, _):
        row = row_of(k)
        for at, device in row[:-1]:
            landed(srecv, at, s_send, s_recv, at).wait_recv()
            s_copy(at, device).wait_send()

        @pl.when(k < NY - 1)
        def _():
            at, device = row[-1]
            landed(srecv, at, s_send, s_recv, at).wait_recv()
            s_copy(at, device).wait_send()

        for at, _ in row:
            finish(at)
        return 0

    lax.fori_loop(0, NY, finish_row, 0)


def exchange(boxes, send_pick, recv_pick, count, markers, velocity):
    vmem = pl.BlockSpec(memory_space=pltpu.VMEM)
    hbm = pl.BlockSpec(memory_space=pltpu.HBM)
    dma = pltpu.SemaphoreType.DMA
    return pl.pallas_call(
        exchange_kernel,
        out_shape=(
            pltpu.VMEM(markers.shape, F32),
            pltpu.VMEM((BUB, CHIPS * LANES), F32),
        ),
        in_specs=[hbm] * 6,
        out_specs=[vmem] * 2,
        scratch_shapes=[
            pltpu.SMEM(boxes.shape, jnp.int32),
            pltpu.VMEM(send_pick.shape, jnp.int32),
            pltpu.VMEM(recv_pick.shape, jnp.int32),
            pltpu.VMEM(count.shape, jnp.int32),
            pltpu.VMEM(markers.shape, F32),
            pltpu.VMEM(velocity.shape, F32),
            pltpu.VMEM((BUB * HALF, LANES), F32),
            pltpu.VMEM((CHIPS, BUB, LANES), BF16),
            pltpu.VMEM((2, LANES), F32),
            pltpu.VMEM((2 * CHIPS, 2, LANES), F32),
            pltpu.VMEM((2 * CHIPS, BUB, LANES), BF16),
            pltpu.VMEM((PAIRS, 256, LANES), BF16),
            pltpu.VMEM((CHIPS, 256), F32),
            pltpu.VMEM((CHIPS, BUB, 2 * LANES), BF16),
            pltpu.VMEM((CHIPS, 256, LANES), F32),
            pltpu.VMEM((CHIPS, BUB, LANES), BF16),
            pltpu.VMEM((CHIPS, BUB, LANES), BF16),
            pltpu.VMEM((2, 4, 64, LANES), F32),
            pltpu.VMEM((2, 64, LANES), F32),
            dma((9,)),
            dma((CHIPS,)),
            dma((CHIPS,)),
            dma((2,)),
            dma((CHIPS,)),
            dma((CHIPS,)),
            dma((NY,)),
            dma((NY,)),
            dma((CHIPS,)),
            dma((CHIPS,)),
            dma((4,)),
            dma((4,)),
        ],
        compiler_params=pltpu.CompilerParams(
            collective_id=0, has_side_effects=True, vmem_limit_bytes=60 * 1024 * 1024
        ),
    )(boxes, send_pick, recv_pick, count, markers, velocity)


def write_kernel(adv, force, adv_out, force_out, sem):
    copies = []
    for i in range(4):
        copies.append(pltpu.make_async_copy(adv.at[i], adv_out.at[i], sem.at[i]))
        part = pl.ds(16 * i, 16)
        copies.append(pltpu.make_async_copy(force.at[part], force_out.at[part], sem.at[4 + i]))
    for copy in copies:
        copy.start()
    for copy in copies:
        copy.wait()


def write(adv, force):
    return pl.pallas_call(
        write_kernel,
        out_shape=(
            jax.ShapeDtypeStruct(adv.shape, F32),
            jax.ShapeDtypeStruct(force.shape, F32),
        ),
        in_specs=[pl.BlockSpec(memory_space=pltpu.VMEM)] * 2,
        out_specs=[pl.BlockSpec(memory_space=pl.ANY)] * 2,
        scratch_shapes=[pltpu.SemaphoreType.DMA((8,))],
        compiler_params=pltpu.CompilerParams(vmem_limit_bytes=16 * 1024 * 1024),
    )(adv, force)


def on_device(markers, velocity, patch_boxes, send_pick, recv_pick, pair_count):
    peers, slots = send_pick.shape[-2:]
    adv, force = exchange(
        patch_boxes,
        send_pick.reshape(peers, slots).T,
        recv_pick.reshape(peers, slots).T,
        pair_count.reshape(1, peers),
        markers,
        velocity,
    )
    return tuple(write(adv, force))


def solution(mesh):
    placed = (
        P(None, "gx", "gy", "gz"),
        P("gx", "gy", "gz"),
        P(None, ("gx", "gy", "gz")),
        P("gx", "gy", "gz", None, None),
        P("gx", "gy", "gz", None, None),
        P("gx", "gy", "gz", None),
    )
    return jax.shard_map(
        on_device,
        mesh=mesh,
        in_specs=placed,
        out_specs=(P(None, "gx", "gy", "gz"), P(("gx", "gy", "gz"), None)),
        check_vma=False,
    )
```

```python
import jax
import jax.numpy as jnp
from jax import lax
from jax.experimental import pallas as pl
from jax.experimental.pallas import tpu as pltpu
from jax.sharding import PartitionSpec as P

MESH = pl.DeviceIdType.MESH
PATCH = 32
BUB = 64
NY = 8
NX = 4
NZ = 12
CHIPS = NX * NY
HALF = CHIPS // 2
PAIRS = CHIPS
LANES = 128
UNUSED = 512.0
ROWS = (4, 3, 5, 2, 6, 1, 7, 0)
F32 = jnp.float32
BF16 = jnp.bfloat16


def iota(shape, dim):
    return lax.broadcasted_iota(jnp.int32, shape, dim)


def chip_at(h):
    y = lax.rem(h, HALF) // 2
    return 2 * lax.rem(h, 2) + lax.rem(h // HALF + y, 2), y


def peer_at(h, core):
    gy, y = chip_at(h)
    return gy * 16 + y * 2 + core


def exchange_kernel(
    boxes_hbm,
    send_hbm,
    recv_hbm,
    count_hbm,
    markers_hbm,
    velocity_hbm,
    adv,
    force,
    boxes,
    send_pick,
    recv_pick,
    count,
    markers,
    velocity,
    tmp,
    ploc,
    x_msg,
    x_all,
    pall,
    fbuf,
    nidx,
    nbuf,
    g,
    ssend,
    srecv,
    mhalo,
    vhalo,
    in_sem,
    x_send,
    x_recv,
    xs_sem,
    p_send,
    p_recv,
    ps_send,
    ps_recv,
    s_send,
    s_recv,
    h_send,
    h_recv,
):
    gx = lax.axis_index("gx")
    gy = lax.axis_index("gy")
    gz = lax.axis_index("gz")
    y = gz // 2
    c = lax.rem(gz, 2)
    parity = lax.rem(gy + y, 2)
    h = parity * HALF + y * 2 + gy // 2
    other = 1 - c
    sibling = (gx, gy, y * 2 + other)
    sides = ((gx < NZ - 1, (gx + 1, gy, gz), 7), (gx > 0, (gx - 1, gy, gz), 0))

    ys = [lax.rem(y + dy, NY) for dy in range(NY)]
    xs = [lax.rem(gy + dx, NX) for dx in range(NX)]
    base = [[lax.rem(parity + i, 2) * HALF + xs[dx] // 2 for dx in range(NX)] for i in range(2)]

    def place(dx, dy):
        number = base[(dx + dy) % 2][dx] + ys[dy] * 2
        return number, (gx, xs[dx], ys[dy] * 2 + c)

    others = [place(dx, dy) for dy in ROWS for dx in (1, 2, 3, 0)][:-1]

    def others_in(half):
        same = parity == half
        even = [jnp.where(same, xs[dx], xs[dx + 1]) for dx in (2, 0)]
        odd = [jnp.where(same, xs[dx + 1], xs[dx]) for dx in (2, 0)]
        found = []
        for dy in ROWS:
            for at in odd if dy % 2 else even:
                found.append((half * HALF + ys[dy] * 2 + at // 2, (gx, at, ys[dy] * 2 + c)))
        return found

    def row_of(k):
        m = 4 - (k + 1) // 2
        ty = lax.rem(y + m + (1 - lax.rem(k, 2)) * (8 - 2 * m), NY)
        odd = lax.rem(ty - y + NY, 2)
        row = []
        for dx in (1, 2, 3, 0):
            at = lax.rem(parity + odd + dx, 2) * HALF + ty * 2 + xs[dx] // 2
            row.append((at, (gx, xs[dx], ty * 2 + c)))
        return row

    barrier = pltpu.get_barrier_semaphore()

    for _, device in others:
        pl.semaphore_signal(barrier, inc=1, device_id=device, device_id_type=MESH)
    pl.semaphore_signal(barrier, inc=1, device_id=sibling, device_id_type=MESH)
    for there, device, _ in sides:

        @pl.when(there)
        def _():
            pl.semaphore_signal(barrier, inc=1, device_id=device, device_id_type=MESH)

    loads = []
    for src, dst in (
        (boxes_hbm, boxes),
        *((markers_hbm.at[m], markers.at[m]) for m in range(4)),
        (send_hbm, send_pick),
        (recv_hbm, recv_pick),
        (count_hbm, count),
        (velocity_hbm, velocity),
    ):
        loads.append(pltpu.make_async_copy(src, dst, in_sem.at[len(loads)]))
    for copy in loads[:-1]:
        copy.start()

    group = iota((8, LANES), 1) // PATCH
    rows = markers.reshape(4 * 8 * 64, LANES)

    def cut(half):
        def one(b, _):
            base = (boxes[0, b] * 8 + boxes[1, b]) * 64 + boxes[2, b]
            z0 = boxes[3, b]
            for dx in range(2):
                cells = None
                for j in range(4):
                    piece = rows[pl.ds(base + (2 * half + dx) * 64 + j, 8, stride=4), :]
                    piece = pltpu.roll(piece, jnp.bitwise_and(PATCH * j - z0 + LANES, LANES - 1), 1)
                    cells = piece if j == 0 else jnp.where(group == j, piece, cells)
                tmp[pl.ds(pl.multiple_of(b * HALF + dx * 8, 8), 8), :] = cells
            return 0

        lax.fori_loop(0, BUB, one, 0, unroll=16)

        def put(s, _):
            ploc[half * HALF + s] = tmp[pl.ds(s, BUB, stride=HALF), :].astype(BF16)
            return 0

        lax.fori_loop(0, HALF, put, 0, unroll=8)

    for copy in loads[:5]:
        copy.wait()
    cut(0)
    loads[-1].start()
    for copy in loads[5:-1]:
        copy.wait()

    for s in range(2):
        far = jnp.where(count[...] > s, send_pick[s : s + 1, :].astype(F32), UNUSED)
        x_msg[s : s + 1, 0:BUB] = far
        x_msg[s : s + 1, BUB:LANES] = recv_pick[s : s + 1, :].astype(F32)

    neighbours = jnp.where(gx < NZ - 1, 1, 0) + jnp.where(gx > 0, 1, 0)
    pl.semaphore_wait(barrier, CHIPS + neighbours)

    def x_copy(to, device):
        return pltpu.make_async_remote_copy(
            src_ref=x_msg,
            dst_ref=x_all.at[c * CHIPS + h],
            send_sem=x_send.at[to],
            recv_sem=x_recv.at[h],
            device_id=device,
            device_id_type=MESH,
        )

    def p_copy(to, device):
        return pltpu.make_async_remote_copy(
            src_ref=ploc.at[to],
            dst_ref=pall.at[c * CHIPS + h],
            send_sem=p_send.at[to],
            recv_sem=p_recv.at[h],
            device_id=device,
            device_id_type=MESH,
        )

    def s_copy(to, device):
        return pltpu.make_async_remote_copy(
            src_ref=ssend.at[to],
            dst_ref=srecv.at[h],
            send_sem=s_send.at[to],
            recv_sem=s_recv.at[h],
            device_id=device,
            device_id_type=MESH,
        )

    def landed(buffer, at, send_sem, recv_sem, frm):
        return pltpu.make_async_remote_copy(
            src_ref=buffer.at[at],
            dst_ref=buffer.at[at],
            send_sem=send_sem.at[frm],
            recv_sem=recv_sem.at[frm],
            device_id=sibling,
            device_id_type=MESH,
        )

    def halo_copies(way):
        _, device, plane = sides[way]
        return (
            pltpu.make_async_remote_copy(
                src_ref=markers.at[:, plane],
                dst_ref=mhalo.at[way],
                send_sem=h_send.at[2 * way],
                recv_sem=h_recv.at[2 * way],
                device_id=device,
                device_id_type=MESH,
            ),
            pltpu.make_async_remote_copy(
                src_ref=velocity.at[plane],
                dst_ref=vhalo.at[way],
                send_sem=h_send.at[2 * way + 1],
                recv_sem=h_recv.at[2 * way + 1],
                device_id=device,
                device_id_type=MESH,
            ),
        )

    def send_half(copy, half):
        found = others_in(half)
        for to, device in found[:-1]:
            copy(to, device).start()

        @pl.when(parity != half)
        def _():
            copy(*found[-1]).start()

    send_half(x_copy, 0)
    send_half(p_copy, 0)
    send_half(x_copy, 1)
    cut(1)
    send_half(p_copy, 1)
    loads[-1].wait()
    for way in range(2):

        @pl.when(sides[way][0])
        def _():
            for copy in halo_copies(way):
                copy.start()

    x_all[c * CHIPS + h] = x_msg[...]
    pall[c * CHIPS + h] = ploc[h]

    row = iota((256, LANES), 0)
    lane = iota((256, LANES), 1)
    from_peer = peer_at(row // 8, c)
    slot = lax.rem(row, 4)
    spread = []
    for s in range(2):
        hit = (lax.rem(slot, 2) == s) & (lane == from_peer + jnp.where(slot < 2, 0, BUB))
        spread.append(jnp.where(hit, 1.0, 0.0).astype(BF16))
    wanted = (lane - BUB * lax.rem(row // 4, 2)).astype(F32)

    row = iota((LANES, 256), 0)
    lane = iota((LANES, 256), 1)
    to_peer = peer_at(lax.rem(lane // 4, CHIPS), lane // LANES)
    slot = lax.rem(lane, 4)
    order = []
    for s in range(2):
        hit = (lax.rem(slot, 2) == s) & (row == to_peer + jnp.where(slot < 2, BUB, 0))
        order.append(jnp.where(hit, 1.0, 0.0).astype(BF16))

    half_row = iota((256, CHIPS), 0)
    half_lane = iota((256, CHIPS), 1)
    pair_half = lax.rem(half_lane, 2) == lax.rem(half_row // 4, 2)
    pair_of = iota((CHIPS, LANES), 0) // 2

    bubble = iota((BUB, 2 * LANES), 0).astype(F32)

    for frm, _ in others:
        landed(x_all, c * CHIPS + frm, x_send, x_recv, frm).wait_recv()
    x_share = pltpu.make_async_remote_copy(
        src_ref=x_all.at[pl.ds(c * CHIPS, CHIPS)],
        dst_ref=x_all.at[pl.ds(c * CHIPS, CHIPS)],
        send_sem=xs_sem.at[0],
        recv_sem=xs_sem.at[1],
        device_id=sibling,
        device_id_type=MESH,
    )
    x_share.start()

    def gather_matrices(core):
        wide = jnp.zeros((256, CHIPS), F32)
        for s in range(2):
            wide += lax.dot_general(
                spread[s],
                x_all[pl.ds(core * CHIPS, CHIPS), s, :].astype(BF16),
                (((1,), (1,)), ((), ())),
                preferred_element_type=F32,
            )
        wide = jnp.where(pair_half, wide, 0.0).astype(BF16)

        def matrix(k, _):
            pick = jnp.where(pair_of == k, 1.0, 0.0).astype(BF16)
            index = jnp.dot(wide, pick, preferred_element_type=F32)
            fbuf[core * HALF + k] = jnp.where(index == wanted, 1.0, 0.0).astype(BF16)
            return 0

        lax.fori_loop(0, HALF, matrix, 0, unroll=8)

    gather_matrices(c)

    index = jnp.zeros((CHIPS, 256), F32)
    for s in range(2):
        index += jnp.dot(
            x_all[pl.ds(c * CHIPS, CHIPS), s, :].astype(BF16),
            order[s],
            preferred_element_type=F32,
        )
    nidx[...] = index

    def sum_matrix(q, _):
        nbuf[q] = jnp.where(bubble == nidx[pl.ds(q, 1), :], 1.0, 0.0).astype(BF16)
        return 0

    lax.fori_loop(0, CHIPS, sum_matrix, 0, unroll=4)

    def gather(core, half):
        for i in range(8):
            pair = core * HALF + half * 8 + i
            patches = pall[pl.ds(2 * pair, 2)].reshape(2 * BUB, LANES)
            partner = jnp.dot(fbuf[pair], patches, preferred_element_type=F32)
            g[:, pl.ds(pl.multiple_of(pair * 8, 8), 8), :] = partner.reshape(CHIPS, 8, LANES)

    def share(core, line):
        chips = pl.ds(core * CHIPS + line * 4, 4)
        return pltpu.make_async_remote_copy(
            src_ref=pall.at[chips],
            dst_ref=pall.at[chips],
            send_sem=ps_send.at[line],
            recv_sem=ps_recv.at[line],
            device_id=sibling,
            device_id_type=MESH,
        )

    def lines(half):
        return [half * 4 + lax.rem(y // 2 + step, 4) for step in (2, 1, 3, 0)]

    for half in range(2):
        for line in lines(half):
            for i in range(4):
                frm = line * 4 + i

                @pl.when(frm != h)
                def _():
                    landed(pall, c * CHIPS + frm, p_send, p_recv, frm).wait_recv()

            share(c, line).start()
        gather(c, half)

    x_share.wait()
    gather_matrices(other)

    for half in range(2):
        for line in lines(half):
            share(other, line).wait_recv()
        gather(other, half)

    def send_s(k, _):
        row = row_of(k)
        for to, _ in row:
            part = jnp.dot(nbuf[to], g[to].astype(BF16), preferred_element_type=F32)
            ssend[to] = part.astype(BF16)
        for to, device in row[:-1]:
            s_copy(to, device).start()

        @pl.when(k < NY - 1)
        def _():
            s_copy(*row[-1]).start()

        return 0

    lax.fori_loop(0, NY, send_s, 0)
    srecv[h] = ssend[h]

    for to, device in others:
        x_copy(to, device).wait_send()
        p_copy(to, device).wait_send()
    for line in range(NY):
        share(c, line).wait_send()

    for way in range(2):

        @pl.when(sides[way][0])
        def _():
            for copy in halo_copies(way):
                copy.wait_send()

        @pl.when(sides[1 - way][0])
        def _():
            for copy in halo_copies(way):
                copy.wait_recv()

        @pl.when(jnp.logical_not(sides[1 - way][0]))
        def _():
            mhalo[way] = jnp.zeros(mhalo.shape[1:], F32)
            vhalo[way] = jnp.zeros(vhalo.shape[1:], F32)


    def advect(t, _):
        rows = pl.ds(pl.multiple_of(t * 8, 8), 8)
        vel = [vhalo[0, rows, :]] + [velocity[i, rows, :] for i in range(8)]
        vel = vel + [vhalo[1, rows, :]]
        face = [0.5 * (vel[i] + vel[i + 1]) for i in range(9)]
        for m in range(4):
            mark = [mhalo[0, m, rows, :]] + [markers[m, i, rows, :] for i in range(8)]
            mark = mark + [mhalo[1, m, rows, :]]
            flux = [face[i] * jnp.where(face[i] > 0, mark[i], mark[i + 1]) for i in range(9)]
            for i in range(8):
                here = mark[i + 1]
                adv[m, i, rows, :] = (
                    here - (flux[i + 1] - flux[i]) + here * (face[i + 1] - face[i])
                )
        return 0

    lax.fori_loop(0, 8, advect, 0)

    def finish(at):
        patch = ploc[at].astype(F32)
        lanes = pl.ds(pl.multiple_of(at * LANES, LANES), LANES)
        force[:, lanes] = 0.8 * patch * (1.0 - patch) * srecv[at].astype(F32)

    def finish_row(k, _):
        row = row_of(k)
        for at, device in row[:-1]:
            landed(srecv, at, s_send, s_recv, at).wait_recv()
            s_copy(at, device).wait_send()

        @pl.when(k < NY - 1)
        def _():
            at, device = row[-1]
            landed(srecv, at, s_send, s_recv, at).wait_recv()
            s_copy(at, device).wait_send()

        for at, _ in row:
            finish(at)
        return 0

    lax.fori_loop(0, NY, finish_row, 0)


def exchange(boxes, send_pick, recv_pick, count, markers, velocity):
    vmem = pl.BlockSpec(memory_space=pltpu.VMEM)
    hbm = pl.BlockSpec(memory_space=pltpu.HBM)
    dma = pltpu.SemaphoreType.DMA
    return pl.pallas_call(
        exchange_kernel,
        out_shape=(
            pltpu.VMEM(markers.shape, F32),
            pltpu.VMEM((BUB, CHIPS * LANES), F32),
        ),
        in_specs=[hbm] * 6,
        out_specs=[vmem] * 2,
        scratch_shapes=[
            pltpu.SMEM(boxes.shape, jnp.int32),
            pltpu.VMEM(send_pick.shape, jnp.int32),
            pltpu.VMEM(recv_pick.shape, jnp.int32),
            pltpu.VMEM(count.shape, jnp.int32),
            pltpu.VMEM(markers.shape, F32),
            pltpu.VMEM(velocity.shape, F32),
            pltpu.VMEM((BUB * HALF, LANES), F32),
            pltpu.VMEM((CHIPS, BUB, LANES), BF16),
            pltpu.VMEM((2, LANES), F32),
            pltpu.VMEM((2 * CHIPS, 2, LANES), F32),
            pltpu.VMEM((2 * CHIPS, BUB, LANES), BF16),
            pltpu.VMEM((PAIRS, 256, LANES), BF16),
            pltpu.VMEM((CHIPS, 256), F32),
            pltpu.VMEM((CHIPS, BUB, 2 * LANES), BF16),
            pltpu.VMEM((CHIPS, 256, LANES), F32),
            pltpu.VMEM((CHIPS, BUB, LANES), BF16),
            pltpu.VMEM((CHIPS, BUB, LANES), BF16),
            pltpu.VMEM((2, 4, 64, LANES), F32),
            pltpu.VMEM((2, 64, LANES), F32),
            dma((9,)),
            dma((CHIPS,)),
            dma((CHIPS,)),
            dma((2,)),
            dma((CHIPS,)),
            dma((CHIPS,)),
            dma((NY,)),
            dma((NY,)),
            dma((CHIPS,)),
            dma((CHIPS,)),
            dma((4,)),
            dma((4,)),
        ],
        compiler_params=pltpu.CompilerParams(
            collective_id=0, has_side_effects=True, vmem_limit_bytes=60 * 1024 * 1024
        ),
    )(boxes, send_pick, recv_pick, count, markers, velocity)


def write_kernel(adv, force, adv_out, force_out, sem):
    copies = []
    for i in range(4):
        copies.append(pltpu.make_async_copy(adv.at[i], adv_out.at[i], sem.at[i]))
        part = pl.ds(16 * i, 16)
        copies.append(pltpu.make_async_copy(force.at[part], force_out.at[part], sem.at[4 + i]))
    for copy in copies:
        copy.start()
    for copy in copies:
        copy.wait()


def write(adv, force):
    return pl.pallas_call(
        write_kernel,
        out_shape=(
            jax.ShapeDtypeStruct(adv.shape, F32),
            jax.ShapeDtypeStruct(force.shape, F32),
        ),
        in_specs=[pl.BlockSpec(memory_space=pltpu.VMEM)] * 2,
        out_specs=[pl.BlockSpec(memory_space=pl.ANY)] * 2,
        scratch_shapes=[pltpu.SemaphoreType.DMA((8,))],
        compiler_params=pltpu.CompilerParams(vmem_limit_bytes=16 * 1024 * 1024),
    )(adv, force)


def on_device(markers, velocity, patch_boxes, send_pick, recv_pick, pair_count):
    peers, slots = send_pick.shape[-2:]
    adv, force = exchange(
        patch_boxes,
        send_pick.reshape(peers, slots).T,
        recv_pick.reshape(peers, slots).T,
        pair_count.reshape(1, peers),
        markers,
        velocity,
    )
    return tuple(write(adv, force))


def solution(mesh):
    placed = (
        P(None, "gx", "gy", "gz"),
        P("gx", "gy", "gz"),
        P(None, ("gx", "gy", "gz")),
        P("gx", "gy", "gz", None, None),
        P("gx", "gy", "gz", None, None),
        P("gx", "gy", "gz", None),
    )
    return jax.shard_map(
        on_device,
        mesh=mesh,
        in_specs=placed,
        out_specs=(P(None, "gx", "gy", "gz"), P(("gx", "gy", "gz"), None)),
        check_vma=False,
    )
```

```python
import jax
import jax.numpy as jnp
from jax import lax
from jax.experimental import pallas as pl
from jax.experimental.pallas import tpu as pltpu
from jax.sharding import PartitionSpec as P

MESH = pl.DeviceIdType.MESH
PATCH = 32
BUB = 64
NY = 8
NX = 4
NZ = 12
CHIPS = NX * NY
HALF = CHIPS // 2
PAIRS = CHIPS
LANES = 128
UNUSED = 512.0
ROWS = (4, 3, 5, 2, 6, 1, 7, 0)
F32 = jnp.float32
BF16 = jnp.bfloat16


def iota(shape, dim):
    return lax.broadcasted_iota(jnp.int32, shape, dim)


def chip_at(h):
    y = lax.rem(h, HALF) // 2
    return 2 * lax.rem(h, 2) + lax.rem(h // HALF + y, 2), y


def peer_at(h, core):
    gy, y = chip_at(h)
    return gy * 16 + y * 2 + core


def exchange_kernel(
    boxes_hbm,
    send_hbm,
    recv_hbm,
    count_hbm,
    markers_hbm,
    velocity_hbm,
    adv,
    force,
    boxes,
    send_pick,
    recv_pick,
    count,
    markers,
    velocity,
    tmp,
    ploc,
    x_msg,
    x_all,
    pall,
    fbuf,
    nidx,
    nbuf,
    g,
    ssend,
    srecv,
    mhalo,
    vhalo,
    in_sem,
    x_send,
    x_recv,
    xs_sem,
    p_send,
    p_recv,
    ps_send,
    ps_recv,
    s_send,
    s_recv,
    h_send,
    h_recv,
):
    gx = lax.axis_index("gx")
    gy = lax.axis_index("gy")
    gz = lax.axis_index("gz")
    y = gz // 2
    c = lax.rem(gz, 2)
    parity = lax.rem(gy + y, 2)
    h = parity * HALF + y * 2 + gy // 2
    other = 1 - c
    sibling = (gx, gy, y * 2 + other)
    sides = ((gx < NZ - 1, (gx + 1, gy, gz), 7), (gx > 0, (gx - 1, gy, gz), 0))

    ys = [lax.rem(y + dy, NY) for dy in range(NY)]
    xs = [lax.rem(gy + dx, NX) for dx in range(NX)]
    base = [[lax.rem(parity + i, 2) * HALF + xs[dx] // 2 for dx in range(NX)] for i in range(2)]

    def place(dx, dy):
        number = base[(dx + dy) % 2][dx] + ys[dy] * 2
        return number, (gx, xs[dx], ys[dy] * 2 + c)

    others = [place(dx, dy) for dy in ROWS for dx in (1, 2, 3, 0)][:-1]

    def others_in(half):
        same = parity == half
        even = [jnp.where(same, xs[dx], xs[dx + 1]) for dx in (2, 0)]
        odd = [jnp.where(same, xs[dx + 1], xs[dx]) for dx in (2, 0)]
        found = []
        for dy in ROWS:
            for at in odd if dy % 2 else even:
                found.append((half * HALF + ys[dy] * 2 + at // 2, (gx, at, ys[dy] * 2 + c)))
        return found

    def row_of(k):
        m = 4 - (k + 1) // 2
        ty = lax.rem(y + m + (1 - lax.rem(k, 2)) * (8 - 2 * m), NY)
        odd = lax.rem(ty - y + NY, 2)
        row = []
        for dx in (1, 2, 3, 0):
            at = lax.rem(parity + odd + dx, 2) * HALF + ty * 2 + xs[dx] // 2
            row.append((at, (gx, xs[dx], ty * 2 + c)))
        return row

    barrier = pltpu.get_barrier_semaphore()

    for _, device in others:
        pl.semaphore_signal(barrier, inc=1, device_id=device, device_id_type=MESH)
    pl.semaphore_signal(barrier, inc=1, device_id=sibling, device_id_type=MESH)
    for there, device, _ in sides:

        @pl.when(there)
        def _():
            pl.semaphore_signal(barrier, inc=1, device_id=device, device_id_type=MESH)

    loads = []
    for src, dst in (
        (boxes_hbm, boxes),
        *((markers_hbm.at[m], markers.at[m]) for m in range(4)),
        (send_hbm, send_pick),
        (recv_hbm, recv_pick),
        (count_hbm, count),
        (velocity_hbm, velocity),
    ):
        loads.append(pltpu.make_async_copy(src, dst, in_sem.at[len(loads)]))
    for copy in loads[:-1]:
        copy.start()

    group = iota((8, LANES), 1) // PATCH
    rows = markers.reshape(4 * 8 * 64, LANES)

    def cut(half):
        def one(b, _):
            base = (boxes[0, b] * 8 + boxes[1, b]) * 64 + boxes[2, b]
            z0 = boxes[3, b]
            for dx in range(2):
                cells = None
                for j in range(4):
                    piece = rows[pl.ds(base + (2 * half + dx) * 64 + j, 8, stride=4), :]
                    piece = pltpu.roll(piece, jnp.bitwise_and(PATCH * j - z0 + LANES, LANES - 1), 1)
                    cells = piece if j == 0 else jnp.where(group == j, piece, cells)
                tmp[pl.ds(pl.multiple_of(b * HALF + dx * 8, 8), 8), :] = cells
            return 0

        lax.fori_loop(0, BUB, one, 0, unroll=16)

        def put(s, _):
            ploc[half * HALF + s] = tmp[pl.ds(s, BUB, stride=HALF), :].astype(BF16)
            return 0

        lax.fori_loop(0, HALF, put, 0, unroll=8)

    for copy in loads[:5]:
        copy.wait()
    cut(0)
    loads[-1].start()
    for copy in loads[5:-1]:
        copy.wait()

    for s in range(2):
        far = jnp.where(count[...] > s, send_pick[s : s + 1, :].astype(F32), UNUSED)
        x_msg[s : s + 1, 0:BUB] = far
        x_msg[s : s + 1, BUB:LANES] = recv_pick[s : s + 1, :].astype(F32)

    neighbours = jnp.where(gx < NZ - 1, 1, 0) + jnp.where(gx > 0, 1, 0)
    pl.semaphore_wait(barrier, CHIPS + neighbours)

    def x_copy(to, device):
        return pltpu.make_async_remote_copy(
            src_ref=x_msg,
            dst_ref=x_all.at[c * CHIPS + h],
            send_sem=x_send.at[to],
            recv_sem=x_recv.at[h],
            device_id=device,
            device_id_type=MESH,
        )

    def p_copy(to, device):
        return pltpu.make_async_remote_copy(
            src_ref=ploc.at[to],
            dst_ref=pall.at[c * CHIPS + h],
            send_sem=p_send.at[to],
            recv_sem=p_recv.at[h],
            device_id=device,
            device_id_type=MESH,
        )

    def s_copy(to, device):
        return pltpu.make_async_remote_copy(
            src_ref=ssend.at[to],
            dst_ref=srecv.at[h],
            send_sem=s_send.at[to],
            recv_sem=s_recv.at[h],
            device_id=device,
            device_id_type=MESH,
        )

    def landed(buffer, at, send_sem, recv_sem, frm):
        return pltpu.make_async_remote_copy(
            src_ref=buffer.at[at],
            dst_ref=buffer.at[at],
            send_sem=send_sem.at[frm],
            recv_sem=recv_sem.at[frm],
            device_id=sibling,
            device_id_type=MESH,
        )

    def halo_copies(way):
        _, device, plane = sides[way]
        return (
            pltpu.make_async_remote_copy(
                src_ref=markers.at[:, plane],
                dst_ref=mhalo.at[way],
                send_sem=h_send.at[2 * way],
                recv_sem=h_recv.at[2 * way],
                device_id=device,
                device_id_type=MESH,
            ),
            pltpu.make_async_remote_copy(
                src_ref=velocity.at[plane],
                dst_ref=vhalo.at[way],
                send_sem=h_send.at[2 * way + 1],
                recv_sem=h_recv.at[2 * way + 1],
                device_id=device,
                device_id_type=MESH,
            ),
        )

    def send_half(copy, half):
        found = others_in(half)
        for to, device in found[:-1]:
            copy(to, device).start()

        @pl.when(parity != half)
        def _():
            copy(*found[-1]).start()

    send_half(x_copy, 0)
    send_half(p_copy, 0)
    send_half(x_copy, 1)
    cut(1)
    send_half(p_copy, 1)
    loads[-1].wait()
    for way in range(2):

        @pl.when(sides[way][0])
        def _():
            for copy in halo_copies(way):
                copy.start()

    x_all[c * CHIPS + h] = x_msg[...]
    pall[c * CHIPS + h] = ploc[h]

    row = iota((256, LANES), 0)
    lane = iota((256, LANES), 1)
    from_peer = peer_at(row // 8, c)
    slot = lax.rem(row, 4)
    spread = []
    for s in range(2):
        hit = (lax.rem(slot, 2) == s) & (lane == from_peer + jnp.where(slot < 2, 0, BUB))
        spread.append(jnp.where(hit, 1.0, 0.0).astype(BF16))
    wanted = (lane - BUB * lax.rem(row // 4, 2)).astype(F32)

    row = iota((LANES, 256), 0)
    lane = iota((LANES, 256), 1)
    to_peer = peer_at(lax.rem(lane // 4, CHIPS), lane // LANES)
    slot = lax.rem(lane, 4)
    order = []
    for s in range(2):
        hit = (lax.rem(slot, 2) == s) & (row == to_peer + jnp.where(slot < 2, BUB, 0))
        order.append(jnp.where(hit, 1.0, 0.0).astype(BF16))

    half_row = iota((256, CHIPS), 0)
    half_lane = iota((256, CHIPS), 1)
    pair_half = lax.rem(half_lane, 2) == lax.rem(half_row // 4, 2)
    pair_of = iota((CHIPS, LANES), 0) // 2

    bubble = iota((BUB, 2 * LANES), 0).astype(F32)

    for frm, _ in others:
        landed(x_all, c * CHIPS + frm, x_send, x_recv, frm).wait_recv()
    x_share = pltpu.make_async_remote_copy(
        src_ref=x_all.at[pl.ds(c * CHIPS, CHIPS)],
        dst_ref=x_all.at[pl.ds(c * CHIPS, CHIPS)],
        send_sem=xs_sem.at[0],
        recv_sem=xs_sem.at[1],
        device_id=sibling,
        device_id_type=MESH,
    )
    x_share.start()

    def gather_matrices(core):
        wide = jnp.zeros((256, CHIPS), F32)
        for s in range(2):
            wide += lax.dot_general(
                spread[s],
                x_all[pl.ds(core * CHIPS, CHIPS), s, :].astype(BF16),
                (((1,), (1,)), ((), ())),
                preferred_element_type=F32,
            )
        wide = jnp.where(pair_half, wide, 0.0).astype(BF16)

        def matrix(k, _):
            pick = jnp.where(pair_of == k, 1.0, 0.0).astype(BF16)
            index = jnp.dot(wide, pick, preferred_element_type=F32)
            fbuf[core * HALF + k] = jnp.where(index == wanted, 1.0, 0.0).astype(BF16)
            return 0

        lax.fori_loop(0, HALF, matrix, 0, unroll=8)

    gather_matrices(c)

    index = jnp.zeros((CHIPS, 256), F32)
    for s in range(2):
        index += jnp.dot(
            x_all[pl.ds(c * CHIPS, CHIPS), s, :].astype(BF16),
            order[s],
            preferred_element_type=F32,
        )
    nidx[...] = index

    def sum_matrix(q, _):
        nbuf[q] = jnp.where(bubble == nidx[pl.ds(q, 1), :], 1.0, 0.0).astype(BF16)
        return 0

    lax.fori_loop(0, CHIPS, sum_matrix, 0, unroll=4)

    def gather(core, half):
        for i in range(8):
            pair = core * HALF + half * 8 + i
            patches = pall[pl.ds(2 * pair, 2)].reshape(2 * BUB, LANES)
            partner = jnp.dot(fbuf[pair], patches, preferred_element_type=F32)
            g[:, pl.ds(pl.multiple_of(pair * 8, 8), 8), :] = partner.reshape(CHIPS, 8, LANES)

    def share(core, line):
        chips = pl.ds(core * CHIPS + line * 4, 4)
        return pltpu.make_async_remote_copy(
            src_ref=pall.at[chips],
            dst_ref=pall.at[chips],
            send_sem=ps_send.at[line],
            recv_sem=ps_recv.at[line],
            device_id=sibling,
            device_id_type=MESH,
        )

    def lines(half):
        return [half * 4 + lax.rem(y // 2 + step, 4) for step in (2, 1, 3, 0)]

    for half in range(2):
        for line in lines(half):
            for i in range(4):
                frm = line * 4 + i

                @pl.when(frm != h)
                def _():
                    landed(pall, c * CHIPS + frm, p_send, p_recv, frm).wait_recv()

            share(c, line).start()

    for half in range(2):
        gather(c, half)

    x_share.wait()
    gather_matrices(other)

    for half in range(2):
        for line in lines(half):
            share(other, line).wait_recv()
        gather(other, half)

    def send_s(k, _):
        row = row_of(k)
        for to, _ in row:
            part = jnp.dot(nbuf[to], g[to].astype(BF16), preferred_element_type=F32)
            ssend[to] = part.astype(BF16)
        for to, device in row[:-1]:
            s_copy(to, device).start()

        @pl.when(k < NY - 1)
        def _():
            s_copy(*row[-1]).start()

        return 0

    lax.fori_loop(0, NY, send_s, 0)
    srecv[h] = ssend[h]

    for to, device in others:
        x_copy(to, device).wait_send()
        p_copy(to, device).wait_send()
    for line in range(NY):
        share(c, line).wait_send()

    for way in range(2):

        @pl.when(sides[way][0])
        def _():
            for copy in halo_copies(way):
                copy.wait_send()

        @pl.when(sides[1 - way][0])
        def _():
            for copy in halo_copies(way):
                copy.wait_recv()

        @pl.when(jnp.logical_not(sides[1 - way][0]))
        def _():
            mhalo[way] = jnp.zeros(mhalo.shape[1:], F32)
            vhalo[way] = jnp.zeros(vhalo.shape[1:], F32)


    def advect(t, _):
        rows = pl.ds(pl.multiple_of(t * 8, 8), 8)
        vel = [vhalo[0, rows, :]] + [velocity[i, rows, :] for i in range(8)]
        vel = vel + [vhalo[1, rows, :]]
        face = [0.5 * (vel[i] + vel[i + 1]) for i in range(9)]
        for m in range(4):
            mark = [mhalo[0, m, rows, :]] + [markers[m, i, rows, :] for i in range(8)]
            mark = mark + [mhalo[1, m, rows, :]]
            flux = [face[i] * jnp.where(face[i] > 0, mark[i], mark[i + 1]) for i in range(9)]
            for i in range(8):
                here = mark[i + 1]
                adv[m, i, rows, :] = (
                    here - (flux[i + 1] - flux[i]) + here * (face[i + 1] - face[i])
                )
        return 0

    lax.fori_loop(0, 8, advect, 0)

    def finish(at):
        patch = ploc[at].astype(F32)
        lanes = pl.ds(pl.multiple_of(at * LANES, LANES), LANES)
        force[:, lanes] = 0.8 * patch * (1.0 - patch) * srecv[at].astype(F32)

    def finish_row(k, _):
        row = row_of(k)
        for at, device in row[:-1]:
            landed(srecv, at, s_send, s_recv, at).wait_recv()
            s_copy(at, device).wait_send()

        @pl.when(k < NY - 1)
        def _():
            at, device = row[-1]
            landed(srecv, at, s_send, s_recv, at).wait_recv()
            s_copy(at, device).wait_send()

        for at, _ in row:
            finish(at)
        return 0

    lax.fori_loop(0, NY, finish_row, 0)


def exchange(boxes, send_pick, recv_pick, count, markers, velocity):
    vmem = pl.BlockSpec(memory_space=pltpu.VMEM)
    hbm = pl.BlockSpec(memory_space=pltpu.HBM)
    dma = pltpu.SemaphoreType.DMA
    return pl.pallas_call(
        exchange_kernel,
        out_shape=(
            pltpu.VMEM(markers.shape, F32),
            pltpu.VMEM((BUB, CHIPS * LANES), F32),
        ),
        in_specs=[hbm] * 6,
        out_specs=[vmem] * 2,
        scratch_shapes=[
            pltpu.SMEM(boxes.shape, jnp.int32),
            pltpu.VMEM(send_pick.shape, jnp.int32),
            pltpu.VMEM(recv_pick.shape, jnp.int32),
            pltpu.VMEM(count.shape, jnp.int32),
            pltpu.VMEM(markers.shape, F32),
            pltpu.VMEM(velocity.shape, F32),
            pltpu.VMEM((BUB * HALF, LANES), F32),
            pltpu.VMEM((CHIPS, BUB, LANES), BF16),
            pltpu.VMEM((2, LANES), F32),
            pltpu.VMEM((2 * CHIPS, 2, LANES), F32),
            pltpu.VMEM((2 * CHIPS, BUB, LANES), BF16),
            pltpu.VMEM((PAIRS, 256, LANES), BF16),
            pltpu.VMEM((CHIPS, 256), F32),
            pltpu.VMEM((CHIPS, BUB, 2 * LANES), BF16),
            pltpu.VMEM((CHIPS, 256, LANES), F32),
            pltpu.VMEM((CHIPS, BUB, LANES), BF16),
            pltpu.VMEM((CHIPS, BUB, LANES), BF16),
            pltpu.VMEM((2, 4, 64, LANES), F32),
            pltpu.VMEM((2, 64, LANES), F32),
            dma((9,)),
            dma((CHIPS,)),
            dma((CHIPS,)),
            dma((2,)),
            dma((CHIPS,)),
            dma((CHIPS,)),
            dma((NY,)),
            dma((NY,)),
            dma((CHIPS,)),
            dma((CHIPS,)),
            dma((4,)),
            dma((4,)),
        ],
        compiler_params=pltpu.CompilerParams(
            collective_id=0, has_side_effects=True, vmem_limit_bytes=60 * 1024 * 1024
        ),
    )(boxes, send_pick, recv_pick, count, markers, velocity)


def write_kernel(adv, force, adv_out, force_out, sem):
    copies = []
    for i in range(4):
        copies.append(pltpu.make_async_copy(adv.at[i], adv_out.at[i], sem.at[i]))
        part = pl.ds(16 * i, 16)
        copies.append(pltpu.make_async_copy(force.at[part], force_out.at[part], sem.at[4 + i]))
    for copy in copies:
        copy.start()
    for copy in copies:
        copy.wait()


def write(adv, force):
    return pl.pallas_call(
        write_kernel,
        out_shape=(
            jax.ShapeDtypeStruct(adv.shape, F32),
            jax.ShapeDtypeStruct(force.shape, F32),
        ),
        in_specs=[pl.BlockSpec(memory_space=pltpu.VMEM)] * 2,
        out_specs=[pl.BlockSpec(memory_space=pl.ANY)] * 2,
        scratch_shapes=[pltpu.SemaphoreType.DMA((8,))],
        compiler_params=pltpu.CompilerParams(vmem_limit_bytes=16 * 1024 * 1024),
    )(adv, force)


def on_device(markers, velocity, patch_boxes, send_pick, recv_pick, pair_count):
    peers, slots = send_pick.shape[-2:]
    adv, force = exchange(
        patch_boxes,
        send_pick.reshape(peers, slots).T,
        recv_pick.reshape(peers, slots).T,
        pair_count.reshape(1, peers),
        markers,
        velocity,
    )
    return tuple(write(adv, force))


def solution(mesh):
    placed = (
        P(None, "gx", "gy", "gz"),
        P("gx", "gy", "gz"),
        P(None, ("gx", "gy", "gz")),
        P("gx", "gy", "gz", None, None),
        P("gx", "gy", "gz", None, None),
        P("gx", "gy", "gz", None),
    )
    return jax.shard_map(
        on_device,
        mesh=mesh,
        in_specs=placed,
        out_specs=(P(None, "gx", "gy", "gz"), P(("gx", "gy", "gz"), None)),
        check_vma=False,
    )
```
